512 devices in a mesh: dir: 16 (over y, z_hi), box: 32 (over x, z_lo, core).
Axes of the slice: x: 4, y: 8, z: 8 (z_hi: 2, z_lo: 4; z = z_hi * 4 + z_lo), core: 2. Of those that a mesh axis runs over, the one named last changes fastest.
Arguments:
- child_fields: bfloat16 [4096, 8, 2, 512], P(('box', 'dir')), may hold values from -6 to 6
- interp_matrix: bfloat16 [512, 2048], replicated, may hold values from -0.25 to 0.25
- phase_angle: float32 [8, 2048], replicated, may hold values from -3.140625 to 3.140625
- patch_order: int32 [32, 128], P('box'), may hold values from 0 to 127, each once within a row
- offset_code: int32 [256, 16, 40], P('box'), may hold values from 0 to 48
- operator_index: int32 [256, 16, 40], P('box'), may hold values from 0 to 127
- operators: bfloat16 [128, 2, 2048], P(None, None, 'dir'), may hold values from -1 to 1
Outputs:
- local_fields: bfloat16 [4096, 8, 2, 512], P(('box', 'dir'))
The draws below stay inside these ranges and needn't reach their ends.
Inputs may be any that keep to these rules, and one draw needn't show every extreme that they name: `patch_order`: each row holds every number of 0 to 127 once. `offset_code`: entry a names the box offset (a // 7 - 3, a % 7 - 3) on the surface grid, whose two dimensions wrap around.
All inputs are finite; a program needn't handle non-finite values.
Results may differ from the reference program's by a relative error of at most 0.0064.
Values may be sent and summed in bfloat16 or wider, within the bound.
No kernel may reach another device: no remote copies, remote signals or barrier semaphores. Data moves between devices by JAX's collectives and lax.ppermute only.
A program may use at most 64 MiB of HBM per device.

```python
import math
import jax
import jax.numpy as jnp
from jax import lax

DC = 512
DP = 2048
CHILDREN = 8
NLIST = 40
NOPS = 128
PV = 16
PB = 128
NPATCH = 32
NU = 256
BOXES = 4096


def place_ends(values, rng, low, high):
    index_at = [jax.random.randint(jax.random.fold_in(rng, axis), (), 0, length) for axis, length in enumerate(values.shape)]
    main_axis = values.shape.index(max(values.shape))
    neighbour = index_at[:main_axis] + [(index_at[main_axis] + 1) % values.shape[main_axis]] + index_at[main_axis + 1:]
    return values.at[tuple(index_at)].set(low).at[tuple(neighbour)].set(high)


def block_levels(own_key, extent, split, smallest, top_value):
    factor_of = 1.0
    for axis_at, parts in split:
        steps = jax.random.uniform(jax.random.fold_in(jax.random.fold_in(own_key, 6), axis_at), (parts,), jnp.float32, smallest / len(split), top_value / len(split))
        factor_of = factor_of * jnp.repeat(jnp.exp(steps), extent[axis_at] // parts).reshape((-1,) + (1,) * (len(extent) - 1 - axis_at))
    return factor_of


def gaussian(rng, shape, width, limit, pieces=(), held_as=jnp.bfloat16):
    factor_of = block_levels(rng, shape, pieces, -0.22, 0.18) if pieces else 1.0
    array = jax.random.normal(rng, shape, jnp.float32) * width * factor_of
    return jnp.minimum(jnp.maximum(array, -limit), limit).astype(held_as)


def setup_inputs(seed: int = 0) -> dict:
    arg_keys = jax.random.split(jax.random.key(seed), 8)
    child_fields = gaussian(arg_keys[0], (BOXES, CHILDREN, 2, DC), 1.0, 6.0, ((0, 512),))
    interp_matrix = gaussian(arg_keys[1], (DC, DP), DC ** -0.5, 0.25)
    phase_angle = jnp.clip(jax.random.uniform(arg_keys[2], (CHILDREN, DP), jnp.float32, -3.140625, 3.140625), -3.140625, 3.140625)
    patch_order = jax.vmap(lambda own: jax.random.permutation(own, PB))(jax.random.split(arg_keys[3], NPATCH)).reshape((NPATCH, PB)).astype(jnp.int32)
    offset_code = place_ends(jax.random.randint(arg_keys[4], (NU, PV, NLIST), 0, 49), jax.random.fold_in(arg_keys[4], 1), 0, 48).astype(jnp.int32)
    operator_index = place_ends(jax.random.randint(arg_keys[5], (NU, PV, NLIST), 0, NOPS), jax.random.fold_in(arg_keys[5], 1), 0, NOPS - 1).astype(jnp.int32)
    operators = gaussian(arg_keys[6], (NOPS, 2, DP), NLIST ** -0.5, 1.0, ((2, 16),))
    return {"child_fields": child_fields, "interp_matrix": interp_matrix, "phase_angle": phase_angle, "patch_order": patch_order, "offset_code": offset_code, "operator_index": operator_index, "operators": operators}


def aggregate_boxes(fields, interp_matrix, cosine_part, sine_part):
    box_count = fields.shape[0]
    flat_rows = fields.reshape(box_count * CHILDREN * 2, DC)
    product = jnp.dot(flat_rows, interp_matrix, preferred_element_type=jnp.float32).reshape(box_count, CHILDREN, 2, DP)
    real_part = jnp.sum(cosine_part * product[:, :, 0] - sine_part * product[:, :, 1], axis=1)
    imaginary_component = jnp.sum(cosine_part * product[:, :, 1] + sine_part * product[:, :, 0], axis=1)
    return jnp.stack([real_part, imaginary_component], axis=1).astype(jnp.bfloat16)


def anterpolate_boxes(fields, interp_matrix, cosine_part, sine_part):
    box_count = fields.shape[0]
    values = fields.astype(jnp.float32)
    shifted_real = cosine_part * values[:, None, 0] + sine_part * values[:, None, 1]
    shifted_imag = cosine_part * values[:, None, 1] - sine_part * values[:, None, 0]
    shifted = jnp.stack([shifted_real, shifted_imag], axis=2).astype(jnp.bfloat16)
    flat_rows = shifted.reshape(box_count * CHILDREN * 2, DP)
    result = lax.dot_general(flat_rows, interp_matrix, (((1,), (1,)), ((), ())), preferred_element_type=jnp.float32)
    return (result * (DC / DP)).astype(jnp.bfloat16).reshape(box_count, CHILDREN, 2, DC)


def translate_band(grid, codes, chosen, ops_band):
    row_ids = jnp.arange(NU, dtype=jnp.int32)[:, None]
    col_ids = jnp.arange(PV, dtype=jnp.int32)[None, :]
    band_width = grid.shape[3]

    def accumulate(totals, inputs):
        entry_code, entry_operator = inputs
        source_row = (row_ids + entry_code // 7 - 3) % NU
        source_col = (col_ids + entry_code % 7 - 3) % PV
        source = grid[source_row, source_col].astype(jnp.float32)
        factor = ops_band[entry_operator].astype(jnp.float32)
        real_total = totals[0] + factor[:, :, 0] * source[:, :, 0] - factor[:, :, 1] * source[:, :, 1]
        imag_total = totals[1] + factor[:, :, 0] * source[:, :, 1] + factor[:, :, 1] * source[:, :, 0]
        return (real_total, imag_total), None

    empty_total = jnp.zeros((NU, PV, band_width), jnp.float32)
    totals, unused = lax.scan(accumulate, (empty_total, empty_total), (codes, chosen))
    return jnp.stack([totals[0], totals[1]], axis=2).astype(jnp.bfloat16)


def reference(child_fields, interp_matrix, phase_angle, patch_order, offset_code, operator_index, operators):
    cosine_part = jnp.cos(phase_angle)
    sine_part = jnp.sin(phase_angle)
    block_boxes = math.gcd(BOXES, 512)

    def aggregate_block(fields):
        return aggregate_boxes(fields, interp_matrix, cosine_part, sine_part)

    def anterpolate_block(fields):
        return anterpolate_boxes(fields, interp_matrix, cosine_part, sine_part)

    def pick_rows(source_rows, order_row):
        return source_rows[order_row]

    def place_rows(values, order_row):
        return jnp.zeros_like(values).at[order_row].set(values)

    blocks = child_fields.reshape(BOXES // block_boxes, block_boxes, CHILDREN, 2, DC)
    parents = lax.map(aggregate_block, blocks).reshape(NPATCH, PB, 2, DP)
    grid = jax.vmap(pick_rows)(parents, patch_order).reshape(NU, PV, 2, DP)

    band_size = 512 if DP % 512 == 0 else DP
    band_count = DP // band_size
    grid_bands = grid.reshape(NU, PV, 2, band_count, band_size).transpose(3, 0, 1, 2, 4)
    ops_bands = operators.reshape(NOPS, 2, band_count, band_size).transpose(2, 0, 1, 3)
    codes = offset_code.transpose(2, 0, 1)
    chosen = operator_index.transpose(2, 0, 1)

    def translate_one(paired):
        return translate_band(paired[0], codes, chosen, paired[1])

    translated = lax.map(translate_one, (grid_bands, ops_bands))
    translated = translated.transpose(1, 2, 3, 0, 4).reshape(NPATCH, PB, 2, DP)
    returned = jax.vmap(place_rows)(translated, patch_order)
    returned = returned.reshape(BOXES // block_boxes, block_boxes, 2, DP)
    local_fields = lax.map(anterpolate_block, returned)
    return local_fields.reshape(BOXES, CHILDREN, 2, DC)
```

```python
import jax
import jax.numpy as jnp
from jax import lax
from jax.experimental import pallas as pl
from jax.experimental.pallas import tpu as pltpu
from jax.sharding import Mesh
from jax.sharding import PartitionSpec as P

DC = 512
DP = 2048
CHILDREN = 8
BAND = 128
CELLS = 128
COLS = 16
ENTRIES = 40
HALO = 48
DIR = ("dir_0", "dir_1")
BOX_DIR = ("box", "dir_0", "dir_1")
F32 = jnp.float32
BF16 = jnp.bfloat16
VMEM_LIMIT = 48 * 1024 * 1024


def params():
    return pltpu.CompilerParams(vmem_limit_bytes=VMEM_LIMIT)


def cos_sin(angle):
    half = angle * 0.5
    sq = half * half
    s = F32(1.0 / 6227020800.0)
    for c in (-1.0 / 39916800.0, 1.0 / 362880.0, -1.0 / 5040.0, 1.0 / 120.0, -1.0 / 6.0, 1.0):
        s = s * sq + F32(c)
    s = s * half
    c_ = F32(1.0 / 479001600.0)
    for c in (-1.0 / 3628800.0, 1.0 / 40320.0, -1.0 / 720.0, 1.0 / 24.0, -0.5, 1.0):
        c_ = c_ * sq + F32(c)
    return 1.0 - 2.0 * s * s, 2.0 * s * c_


def aggregate_kernel(child_ref, interp_ref, phase_ref, out_ref):
    c, s = cos_sin(phase_ref[...])
    prod = jnp.dot(child_ref[...], interp_ref[...], preferred_element_type=F32)
    re = jnp.zeros((8, prod.shape[1]), F32)
    im = re
    for k in range(CHILDREN):
        pr, pi = prod[8 * k : 8 * k + 8], prod[64 + 8 * k : 72 + 8 * k]
        ck, sk = c[k : k + 1], s[k : k + 1]
        re = re + (ck * pr - sk * pi)
        im = im + (ck * pi + sk * pr)
    blocks = []
    for d in range(prod.shape[1] // BAND):
        at = slice(d * BAND, (d + 1) * BAND)
        blocks.append(jnp.concatenate([re[:, at], im[:, at]], axis=1))
    out_ref[...] = jnp.concatenate(blocks, axis=0).astype(BF16)


def aggregate(child_rows, interp, phase):
    tile = 512
    return pl.pallas_call(
        aggregate_kernel,
        grid=(DP // tile,),
        in_specs=[
            pl.BlockSpec((128, DC), lambda i: (0, 0)),
            pl.BlockSpec((DC, tile), lambda i: (0, i)),
            pl.BlockSpec((CHILDREN, tile), lambda i: (0, i)),
        ],
        out_specs=pl.BlockSpec((8 * tile // BAND, 2 * BAND), lambda i: (i, 0)),
        out_shape=jax.ShapeDtypeStruct((8 * DP // BAND, 2 * BAND), BF16),
        compiler_params=params(),
        cost_estimate=pl.CostEstimate(flops=2 * 128 * DC * DP, bytes_accessed=DC * DP * 2, transcendentals=0),
    )(child_rows, interp, phase)


def placement(order_row):
    rows = lax.broadcasted_iota(jnp.int32, (CELLS, CELLS), 0)
    return jnp.where(rows == order_row, 1.0, 0.0)


def cells_kernel(listed_ref, order_ref, cells_ref, low_ref, high_ref):
    onehot = placement(order_ref[...]).T.astype(BF16)
    cells = jnp.dot(onehot, listed_ref[...], preferred_element_type=F32).astype(BF16)
    cells_ref[...] = cells
    low_ref[...] = cells[:HALO]
    high_ref[...] = cells[CELLS - HALO :]


def to_cells(listed, order):
    edge = jax.ShapeDtypeStruct((HALO, 2 * BAND), BF16)
    return pl.pallas_call(
        cells_kernel,
        out_shape=(jax.ShapeDtypeStruct((CELLS, 2 * BAND), BF16), edge, edge),
        compiler_params=params(),
    )(listed, order)


def operators_kernel(index_ref, ops_ref, out_ref):
    index = index_ref[...]
    lanes = lax.broadcasted_iota(jnp.int32, (CELLS, BAND), 1)
    ops = ops_ref[...]
    step = 8
    for j0 in range(0, ENTRIES, step):
        picks = [
            jnp.where(index[:, j : j + 1] == lanes, 1.0, 0.0).astype(BF16)
            for j in range(j0, j0 + step)
        ]
        chosen = jnp.dot(jnp.concatenate(picks, axis=0), ops, preferred_element_type=F32)
        out_ref[j0 * CELLS : (j0 + step) * CELLS] = chosen.astype(BF16)


def chosen_operators(index, ops):
    return pl.pallas_call(
        operators_kernel,
        out_shape=jax.ShapeDtypeStruct((ENTRIES * CELLS, 2 * BAND), BF16),
        compiler_params=params(),
        cost_estimate=pl.CostEstimate(
            flops=2 * ENTRIES * CELLS * 128 * 256, bytes_accessed=ENTRIES * CELLS * 512, transcendentals=0
        ),
    )(index, ops)


def translate_kernel(cells_ref, before_ref, after_ref, code_ref, chosen_ref, order_ref, out_ref):
    grid_rows = jnp.concatenate([before_ref[...], cells_ref[...], after_ref[...]], axis=0)
    code = code_ref[...]
    cell = lax.broadcasted_iota(jnp.int32, code.shape, 0)
    up = (code * 37) >> 8
    source = ((cell >> 4) + up) * COLS + (((cell & 15) + code - 7 * up + (COLS - 3)) & 15)
    total_rows = CELLS + 2 * HALO
    lanes = lax.broadcasted_iota(jnp.int32, (CELLS, total_rows), 1)
    re = jnp.zeros((CELLS, BAND), F32)
    im = re
    step = 8
    for j0 in range(0, ENTRIES, step):
        picks = [
            jnp.where(source[:, j : j + 1] == lanes, 1.0, 0.0).astype(BF16)
            for j in range(j0, j0 + step)
        ]
        got = jnp.dot(jnp.concatenate(picks, axis=0), grid_rows, preferred_element_type=F32)
        for k in range(step):
            op = chosen_ref[(j0 + k) * CELLS : (j0 + k + 1) * CELLS].astype(F32)
            g = got[k * CELLS : (k + 1) * CELLS]
            gr, gi, wr, wi = g[:, :BAND], g[:, BAND:], op[:, :BAND], op[:, BAND:]
            re = re + (wr * gr - wi * gi)
            im = im + (wr * gi + wi * gr)
    translated = jnp.concatenate([re, im], axis=1).astype(BF16)
    onehot = placement(order_ref[...]).astype(BF16)
    out_ref[...] = jnp.dot(onehot, translated, preferred_element_type=F32).astype(BF16)


def translate(cells, before, after, code, chosen, order):
    return pl.pallas_call(
        translate_kernel,
        out_shape=jax.ShapeDtypeStruct((CELLS, 2 * BAND), BF16),
        compiler_params=params(),
    )(cells, before, after, code, chosen, order)


def anterpolate_kernel(recv_ref, interp_ref, phase_ref, out_ref, total_ref):
    step = pl.program_id(0)
    c, s = cos_sin(phase_ref[...])
    values = recv_ref[...].astype(F32)
    blocks = values.shape[0] // 8
    re = jnp.concatenate([values[8 * d : 8 * d + 8, :BAND] for d in range(blocks)], axis=1)
    im = jnp.concatenate([values[8 * d : 8 * d + 8, BAND:] for d in range(blocks)], axis=1)
    real, imag = [], []
    for k in range(CHILDREN):
        ck, sk = c[k : k + 1], s[k : k + 1]
        real.append(ck * re + sk * im)
        imag.append(ck * im - sk * re)
    shifted = jnp.concatenate(real + imag, axis=0).astype(BF16)
    part = lax.dot_general(shifted, interp_ref[...], (((1,), (1,)), ((), ())), preferred_element_type=F32)

    @pl.when(step == 0)
    def _():
        total_ref[...] = part

    @pl.when(step > 0)
    def _():
        total_ref[...] += part

    @pl.when(step == pl.num_programs(0) - 1)
    def _():
        out_ref[...] = (total_ref[...] * (DC / DP)).astype(BF16)


def anterpolate(received, interp, phase):
    tile = 512
    return pl.pallas_call(
        anterpolate_kernel,
        grid=(DP // tile,),
        in_specs=[
            pl.BlockSpec((8 * tile // BAND, 2 * BAND), lambda i: (i, 0)),
            pl.BlockSpec((DC, tile), lambda i: (0, i)),
            pl.BlockSpec((CHILDREN, tile), lambda i: (0, i)),
        ],
        out_specs=pl.BlockSpec((128, DC), lambda i: (0, 0)),
        out_shape=jax.ShapeDtypeStruct((128, DC), BF16),
        scratch_shapes=[pltpu.VMEM((128, DC), F32)],
        compiler_params=params(),
    )(received, interp, phase)


def exchange(rows):
    return lax.all_to_all(rows.reshape(16, 8, 2 * BAND), DIR, 0, 0, tiled=True).reshape(CELLS, 2 * BAND)


def per_device(child_fields, interp_matrix, phase_angle, patch_order, offset_code, operator_index, operators):
    child_rows = child_fields.transpose(2, 1, 0, 3).reshape(128, DC)
    parent = aggregate(child_rows, interp_matrix, phase_angle)
    listed = exchange(parent)
    chosen = chosen_operators(operator_index.reshape(CELLS, ENTRIES), operators.reshape(128, 2 * BAND))
    cells, low, high = to_cells(listed, patch_order)
    size = lax.axis_size("box")
    up = [(i, (i + 1) % size) for i in range(size)]
    down = [(j, i) for i, j in up]
    before = lax.ppermute(high, "box", up)
    after = lax.ppermute(low, "box", down)
    returned = translate(cells, before, after, offset_code.reshape(CELLS, ENTRIES), chosen, patch_order)
    received = exchange(returned)
    fields = anterpolate(received, interp_matrix, phase_angle)
    return fields.reshape(2, CHILDREN, 8, DC).transpose(2, 1, 0, 3)


def solution(mesh):
    split = Mesh(mesh.devices.reshape(8, 2, mesh.shape["box"]), ("dir_0", "dir_1", "box"))
    placed = (
        P(BOX_DIR, None, None, None),
        P(),
        P(),
        P("box", None),
        P("box", None, None),
        P("box", None, None),
        P(None, None, DIR),
    )
    return jax.shard_map(
        per_device,
        mesh=split,
        in_specs=placed,
        out_specs=P(BOX_DIR, None, None, None),
        check_vma=False,
    )
```

```python
import jax
import jax.numpy as jnp
from jax import lax
from jax.experimental import pallas as pl
from jax.experimental.pallas import tpu as pltpu
from jax.sharding import Mesh
from jax.sharding import PartitionSpec as P

DC = 512
DP = 2048
CHILDREN = 8
BAND = 128
CELLS = 128
COLS = 16
ENTRIES = 40
DBLOCKS = 16
RUN = 4
DIR = ("dir_0", "dir_1")
F32 = jnp.float32
BF16 = jnp.bfloat16
VMEM_LIMIT = 24 * 1024 * 1024


def params():
    return pltpu.CompilerParams(vmem_limit_bytes=VMEM_LIMIT)


def cos_sin(angle):
    half = angle * 0.5
    sq = half * half
    s = F32(1.0 / 6227020800.0)
    for c in (-1.0 / 39916800.0, 1.0 / 362880.0, -1.0 / 5040.0, 1.0 / 120.0, -1.0 / 6.0, 1.0):
        s = s * sq + F32(c)
    s = s * half
    c_ = F32(1.0 / 479001600.0)
    for c in (-1.0 / 3628800.0, 1.0 / 40320.0, -1.0 / 720.0, 1.0 / 24.0, -0.5, 1.0):
        c_ = c_ * sq + F32(c)
    return 1.0 - 2.0 * s * s, 2.0 * s * c_


def parents(child, interp_ref, phase_ref):
    blocks = []
    tile = 512
    for t in range(DP // tile):
        at = slice(t * tile, (t + 1) * tile)
        c, s = cos_sin(phase_ref[:, at])
        prod = jnp.dot(child, interp_ref[:, at], preferred_element_type=F32)
        re = jnp.zeros((8, tile), F32)
        im = re
        for k in range(CHILDREN):
            pr, pi = prod[8 * k : 8 * k + 8], prod[64 + 8 * k : 72 + 8 * k]
            ck, sk = c[k : k + 1], s[k : k + 1]
            re = re + (ck * pr - sk * pi)
            im = im + (ck * pi + sk * pr)
        for d in range(tile // BAND):
            own = slice(d * BAND, (d + 1) * BAND)
            blocks.append(jnp.concatenate([re[:, own], im[:, own]], axis=1))
    return blocks


def own_kernel(packed_ref, interp_ref, phase_ref, out_ref):
    blocks = parents(packed_ref[:128], interp_ref, phase_ref)
    for d in range(0, DBLOCKS, 2):
        out_ref[8 * d : 8 * d + 16] = jnp.concatenate(blocks[d : d + 2], axis=0).astype(BF16)


def send_kernel(packed_ref, own_ref, order_ref, interp_ref, phase_ref, out_ref):
    core = lax.axis_index("core")
    blocks = parents(packed_ref[:128], interp_ref, phase_ref)
    order = order_ref[...].astype(F32)
    order = jnp.broadcast_to(jnp.concatenate([order, order], axis=1), (8, 2 * BAND))
    own = own_ref[...].astype(F32)
    for d in range(DBLOCKS):
        first = own[8 * d : 8 * d + 8]
        for c in range(2):
            second = jnp.where(core == c, blocks[d], order)
            out_ref[d, c] = jnp.concatenate([first, second], axis=0).astype(BF16)


def whole():
    return pl.BlockSpec(memory_space=pltpu.VMEM)


def own_parents(packed, interp, phase):
    return pl.pallas_call(
        own_kernel,
        in_specs=[whole()] * 3,
        out_specs=whole(),
        out_shape=jax.ShapeDtypeStruct((8 * DBLOCKS, 2 * BAND), BF16),
        compiler_params=params(),
        cost_estimate=pl.CostEstimate(flops=2 * 128 * DC * DP, bytes_accessed=DC * DP * 2, transcendentals=0),
    )(packed, interp, phase)


def to_send(packed, own, order, interp, phase):
    return pl.pallas_call(
        send_kernel,
        in_specs=[whole()] * 5,
        out_specs=whole(),
        out_shape=jax.ShapeDtypeStruct((DBLOCKS, 2, 16, 2 * BAND), BF16),
        compiler_params=params(),
        cost_estimate=pl.CostEstimate(flops=2 * 128 * DC * DP, bytes_accessed=DC * DP * 2, transcendentals=0),
    )(packed, own, order, interp, phase)


def operators_kernel(index_ref, ops_ref, out_ref):
    index = index_ref[...]
    lanes = lax.broadcasted_iota(jnp.int32, (CELLS, BAND), 1)
    ops = ops_ref[...]
    step = 8
    for j0 in range(0, ENTRIES, step):
        picks = [
            jnp.where(index[:, j : j + 1] == lanes, 1.0, 0.0).astype(BF16)
            for j in range(j0, j0 + step)
        ]
        chosen = jnp.dot(jnp.concatenate(picks, axis=0), ops, preferred_element_type=F32)
        out_ref[j0 * CELLS : (j0 + step) * CELLS] = chosen.astype(BF16)


def chosen_operators(index, ops):
    return pl.pallas_call(
        operators_kernel,
        in_specs=[whole()] * 2,
        out_specs=whole(),
        out_shape=jax.ShapeDtypeStruct((ENTRIES * CELLS, 2 * BAND), BF16),
        compiler_params=params(),
        cost_estimate=pl.CostEstimate(
            flops=2 * ENTRIES * CELLS * 128 * 256, bytes_accessed=ENTRIES * CELLS * 512, transcendentals=0
        ),
    )(index, ops)


def translate_kernel(recv_ref, packed_ref, code_ref, chosen_ref, order_ref, out_ref):
    core, chip = lax.axis_index("core"), lax.axis_index("chip")
    flip = jnp.where(core == 0, jnp.where(chip % RUN == 0, 8, 0), jnp.where(chip % RUN == RUN - 1, 8, 0))
    own = order_ref[...]
    mates = [recv_ref[0, c].astype(F32)[8:9, :BAND] for c in range(2)]
    mate = jnp.where(core == 0, mates[1], mates[0]).astype(jnp.int32)
    outside = packed_ref[128:144].astype(F32)[0:1, :BAND].astype(jnp.int32)

    def row_of(position, c, half):
        return (position >> 3) * 32 + c * 16 + half * 8 + (position & 7)

    inside_row = row_of(own, core, 0)
    mate_row = row_of(mate, 1 - core, 0)
    outside_row = row_of(outside ^ flip, core, 1)
    lane = lax.broadcasted_iota(jnp.int32, (1, BAND), 1)
    edge_row = jnp.where((lane < 64) == (core == 0), mate_row, outside_row)
    onehots = []
    for rows in (inside_row, edge_row):
        column = jnp.broadcast_to(rows.astype(F32), (BAND, BAND)).T.astype(jnp.int32)
        parts = [
            jnp.where(column == lax.broadcasted_iota(jnp.int32, (BAND, BAND), 1) + k * BAND, 1.0, 0.0).astype(BF16)
            for k in range(4)
        ]
        onehots.append(jnp.concatenate(parts, axis=1))
    listed = recv_ref[...].reshape(32 * DBLOCKS, 2 * BAND)
    sources = jnp.dot(jnp.concatenate(onehots, axis=0), listed, preferred_element_type=F32).astype(BF16)

    code = code_ref[...]
    cell = lax.broadcasted_iota(jnp.int32, code.shape, 0)
    up = (code * 37) >> 8
    u = (cell >> 4) + up - 3
    v = ((cell & 15) + code - 7 * up + (COLS - 3)) & 15
    source = (u & 7) * COLS + v + jnp.where((u < 0) | (u > 7), CELLS, 0)
    lanes = lax.broadcasted_iota(jnp.int32, (CELLS, 2 * CELLS), 1)
    re = jnp.zeros((CELLS, BAND), F32)
    im = re
    step = 8
    for j0 in range(0, ENTRIES, step):
        picks = [
            jnp.where(source[:, j : j + 1] == lanes, 1.0, 0.0).astype(BF16)
            for j in range(j0, j0 + step)
        ]
        got = jnp.dot(jnp.concatenate(picks, axis=0), sources, preferred_element_type=F32)
        for k in range(step):
            op = chosen_ref[(j0 + k) * CELLS : (j0 + k + 1) * CELLS].astype(F32)
            g = got[k * CELLS : (k + 1) * CELLS]
            gr, gi, wr, wi = g[:, :BAND], g[:, BAND:], op[:, :BAND], op[:, BAND:]
            re = re + (wr * gr - wi * gi)
            im = im + (wr * gi + wi * gr)
    translated = jnp.concatenate([re, im], axis=1).astype(BF16)
    rows = lax.broadcasted_iota(jnp.int32, (CELLS, CELLS), 0)
    onehot = jnp.where(rows == own, 1.0, 0.0).astype(BF16)
    out_ref[...] = jnp.dot(onehot, translated, preferred_element_type=F32).astype(BF16)


def translate(received, packed, code, chosen, order):
    return pl.pallas_call(
        translate_kernel,
        in_specs=[whole()] * 5,
        out_specs=whole(),
        out_shape=jax.ShapeDtypeStruct((CELLS, 2 * BAND), BF16),
        compiler_params=params(),
    )(received, packed, code, chosen, order)


def anterpolate_kernel(recv_ref, interp_ref, phase_ref, out_ref):
    tile = 512
    total = jnp.zeros((128, DC), F32)
    for t in range(DP // tile):
        at = slice(t * tile, (t + 1) * tile)
        c, s = cos_sin(phase_ref[:, at])
        values = recv_ref[8 * tile // BAND * t : 8 * tile // BAND * (t + 1)].astype(F32)
        blocks = values.shape[0] // 8
        re = jnp.concatenate([values[8 * d : 8 * d + 8, :BAND] for d in range(blocks)], axis=1)
        im = jnp.concatenate([values[8 * d : 8 * d + 8, BAND:] for d in range(blocks)], axis=1)
        real, imag = [], []
        for k in range(CHILDREN):
            ck, sk = c[k : k + 1], s[k : k + 1]
            real.append(ck * re + sk * im)
            imag.append(ck * im - sk * re)
        shifted = jnp.concatenate(real + imag, axis=0).astype(BF16)
        total += lax.dot_general(
            shifted, interp_ref[:, at], (((1,), (1,)), ((), ())), preferred_element_type=F32
        )
    out_ref[...] = (total * (DC / DP)).astype(BF16)


def anterpolate(received, interp, phase):
    return pl.pallas_call(
        anterpolate_kernel,
        in_specs=[whole()] * 3,
        out_specs=whole(),
        out_shape=jax.ShapeDtypeStruct((128, DC), BF16),
        compiler_params=params(),
    )(received, interp, phase)


def outside_pairs(halves, chips):
    pairs = []
    for half in range(halves):
        for chip in range(chips):
            there = half ^ 1 if chip % RUN == RUN - 1 else half
            i = (half * chips + chip) * 2 + 1
            j = (there * chips + (chip + 1) % chips) * 2
            pairs += [(i, j), (j, i)]
    return pairs


def per_device(child_fields, interp_matrix, phase_angle, patch_order, offset_code, operator_index, operators):
    child_rows = child_fields.transpose(2, 1, 0, 3).reshape(128, DC)
    order_rows = jnp.pad(patch_order.astype(BF16), ((0, 15), (0, DC - CELLS)))
    packed = jnp.concatenate([child_rows, order_rows], axis=0)
    outside = lax.ppermute(packed, ("dir_1", "chip", "core"), outside_pairs(2, lax.axis_size("chip")))
    own = own_parents(packed, interp_matrix, phase_angle)
    chosen = chosen_operators(operator_index.reshape(CELLS, ENTRIES), operators.reshape(128, 2 * BAND))
    send = to_send(outside, own, patch_order, interp_matrix, phase_angle)
    send, chosen = lax.optimization_barrier((send, chosen))
    listed = lax.all_to_all(send.reshape(2 * DBLOCKS, 16, 2 * BAND), DIR + ("core",), 0, 0, tiled=True)
    returned = translate(
        listed.reshape(DBLOCKS, 2, 16, 2 * BAND), outside, offset_code.reshape(CELLS, ENTRIES), chosen, patch_order
    )
    received = lax.all_to_all(returned.reshape(DBLOCKS, 8, 2 * BAND), DIR, 0, 0, tiled=True)
    fields = anterpolate(received.reshape(8 * DBLOCKS, 2 * BAND), interp_matrix, phase_angle)
    return fields.reshape(2, CHILDREN, 8, DC).transpose(2, 1, 0, 3)


def solution(mesh):
    split = Mesh(mesh.devices.reshape(8, 2, mesh.shape["box"] // 2, 2), ("dir_0", "dir_1", "chip", "core"))
    box = ("chip", "core")
    placed = (
        P(box + DIR, None, None, None),
        P(),
        P(),
        P(box, None),
        P(box, None, None),
        P(box, None, None),
        P(None, None, DIR),
    )
    return jax.shard_map(
        per_device,
        mesh=split,
        in_specs=placed,
        out_specs=P(box + DIR, None, None, None),
        check_vma=False,
    )
```

```python
import jax
import jax.numpy as jnp
from jax import lax
from jax.experimental import pallas as pl
from jax.experimental.pallas import tpu as pltpu
from jax.sharding import Mesh
from jax.sharding import PartitionSpec as P

DC = 512
DP = 2048
CHILDREN = 8
BAND = 128
CELLS = 128
COLS = 16
ENTRIES = 40
DBLOCKS = 16
RUN = 4
TILE = 512
TILES = DP // TILE
DIR = ("dir_0", "dir_1")
F32 = jnp.float32
BF16 = jnp.bfloat16
VMEM_LIMIT = 24 * 1024 * 1024


def params():
    return pltpu.CompilerParams(vmem_limit_bytes=VMEM_LIMIT)


def cos_sin(angle):
    half = angle * 0.5
    sq = half * half
    s = F32(1.0 / 6227020800.0)
    for c in (-1.0 / 39916800.0, 1.0 / 362880.0, -1.0 / 5040.0, 1.0 / 120.0, -1.0 / 6.0, 1.0):
        s = s * sq + F32(c)
    s = s * half
    c_ = F32(1.0 / 479001600.0)
    for c in (-1.0 / 3628800.0, 1.0 / 40320.0, -1.0 / 720.0, 1.0 / 24.0, -0.5, 1.0):
        c_ = c_ * sq + F32(c)
    return 1.0 - 2.0 * s * s, 2.0 * s * c_


def block_fields(child, interp, c, s):
    prod = jnp.dot(child, interp, preferred_element_type=F32)
    re = jnp.zeros((8, prod.shape[1]), F32)
    im = re
    for k in range(CHILDREN):
        pr, pi = prod[8 * k : 8 * k + 8], prod[64 + 8 * k : 72 + 8 * k]
        ck, sk = c[k : k + 1], s[k : k + 1]
        re = re + (ck * pr - sk * pi)
        im = im + (ck * pi + sk * pr)
    columns = [slice(d * BAND, (d + 1) * BAND) for d in range(prod.shape[1] // BAND)]
    return [jnp.concatenate([re[:, at], im[:, at]], axis=1) for at in columns]


def whole():
    return pl.BlockSpec(memory_space=pltpu.VMEM)


def outer():
    return pl.BlockSpec(memory_space=pltpu.HBM)


def pack_kernel(rows_ref, order_ref, out_ref):
    out_ref[:128] = rows_ref[...]
    order = jnp.broadcast_to(order_ref[...].astype(F32), (16, CELLS)).astype(BF16)
    out_ref[128:144] = jnp.concatenate([order] * (DC // CELLS), axis=1)


def pack(rows, order):
    return pl.pallas_call(
        pack_kernel,
        in_specs=[whole()] * 2,
        out_specs=whole(),
        out_shape=jax.ShapeDtypeStruct((144, DC), BF16),
        compiler_params=params(),
    )(rows, order)


def front_kernel(
    packed_ref,
    ops_ref,
    index_hbm,
    interp_hbm,
    phase_hbm,
    own_ref,
    chosen_ref,
    interp_ref,
    cos_ref,
    sin_ref,
    index_ref,
    phase_ref,
    sems,
):
    load_index = pltpu.make_async_copy(index_hbm, index_ref, sems.at[TILES + 1])
    load_index.start()
    load_phase = pltpu.make_async_copy(phase_hbm, phase_ref, sems.at[TILES])
    load_phase.start()
    loads = []
    for t in range(TILES):
        at = pl.ds(t * TILE, TILE)
        loads.append(pltpu.make_async_copy(interp_hbm.at[:, at], interp_ref.at[:, at], sems.at[t]))
        loads[t].start()
    load_index.wait()
    index = index_ref[...]
    lanes = lax.broadcasted_iota(jnp.int32, (CELLS, BAND), 1)
    ops = ops_ref[...]
    step = 8
    for j0 in range(0, ENTRIES, step):
        picks = [
            jnp.where(index[:, j : j + 1] == lanes, 1.0, 0.0).astype(BF16)
            for j in range(j0, j0 + step)
        ]
        chosen = jnp.dot(jnp.concatenate(picks, axis=0), ops, preferred_element_type=F32)
        chosen_ref[j0 * CELLS : (j0 + step) * CELLS] = chosen.astype(BF16)
    load_phase.wait()
    c, s = cos_sin(phase_ref[...])
    cos_ref[...] = c
    sin_ref[...] = s
    child = packed_ref[:128]
    for t in range(TILES):
        at = slice(t * TILE, (t + 1) * TILE)
        loads[t].wait()
        blocks = block_fields(child, interp_ref[:, at], c[:, at], s[:, at])
        rows = 8 * len(blocks)
        own_ref[t * rows : (t + 1) * rows] = jnp.concatenate(blocks, axis=0).astype(BF16)


def front(packed, ops, *outside):
    outside = [pltpu.with_memory_space_constraint(x, pltpu.HBM) for x in outside]
    wave = jax.ShapeDtypeStruct((CHILDREN, DP), F32)
    return pl.pallas_call(
        front_kernel,
        in_specs=[whole()] * 2 + [outer()] * 3,
        out_specs=[whole()] * 5,
        out_shape=(
            jax.ShapeDtypeStruct((8 * DBLOCKS, 2 * BAND), BF16),
            jax.ShapeDtypeStruct((ENTRIES * CELLS, 2 * BAND), BF16),
            jax.ShapeDtypeStruct((DC, DP), BF16),
            wave,
            wave,
        ),
        scratch_shapes=[
            pltpu.VMEM((CELLS, ENTRIES), jnp.int32),
            pltpu.VMEM((CHILDREN, DP), F32),
            pltpu.SemaphoreType.DMA((TILES + 2,)),
        ],
        compiler_params=params(),
        cost_estimate=pl.CostEstimate(flops=4 * 128 * DC * DP, bytes_accessed=DC * DP * 2, transcendentals=0),
    )(packed, ops, *outside)


def send_kernel(packed_ref, own_ref, order_ref, interp_ref, cos_ref, sin_ref, out_ref):
    core = lax.axis_index("core")
    order = order_ref[...].astype(F32)
    order = jnp.broadcast_to(jnp.concatenate([order, order], axis=1), (8, 2 * BAND))
    own = own_ref[...].astype(F32)
    child = packed_ref[:128]
    for t in range(TILES):
        at = slice(t * TILE, (t + 1) * TILE)
        blocks = block_fields(child, interp_ref[:, at], cos_ref[:, at], sin_ref[:, at])
        for k, block in enumerate(blocks):
            d = t * len(blocks) + k
            first = own[8 * d : 8 * d + 8]
            for c in range(2):
                second = jnp.where(core == c, block, order)
                out_ref[d, c] = jnp.concatenate([first, second], axis=0).astype(BF16)


def to_send(packed, own, order, interp, c, s):
    return pl.pallas_call(
        send_kernel,
        in_specs=[whole()] * 6,
        out_specs=whole(),
        out_shape=jax.ShapeDtypeStruct((DBLOCKS, 2, 16, 2 * BAND), BF16),
        compiler_params=params(),
        cost_estimate=pl.CostEstimate(flops=2 * 128 * DC * DP, bytes_accessed=DC * DP * 2, transcendentals=0),
    )(packed, own, order, interp, c, s)


def translate_kernel(recv_ref, packed_ref, code_ref, chosen_ref, order_ref, out_ref):
    core, chip = lax.axis_index("core"), lax.axis_index("chip")
    flip = jnp.where(core == 0, jnp.where(chip % RUN == 0, 8, 0), jnp.where(chip % RUN == RUN - 1, 8, 0))
    own = order_ref[...]
    mates = [recv_ref[0, c].astype(F32)[8:9, :BAND] for c in range(2)]
    mate = jnp.where(core == 0, mates[1], mates[0]).astype(jnp.int32)
    outside = packed_ref[128:144].astype(F32)[0:1, :BAND].astype(jnp.int32)

    def row_of(position, c, half):
        return (position >> 3) * 32 + c * 16 + half * 8 + (position & 7)

    inside_row = row_of(own, core, 0)
    mate_row = row_of(mate, 1 - core, 0)
    outside_row = row_of(outside ^ flip, core, 1)
    lane = lax.broadcasted_iota(jnp.int32, (1, BAND), 1)
    edge_row = jnp.where((lane < 64) == (core == 0), mate_row, outside_row)
    onehots = []
    for rows in (inside_row, edge_row):
        column = jnp.broadcast_to(rows.astype(F32), (BAND, BAND)).T.astype(jnp.int32)
        parts = [
            jnp.where(column == lax.broadcasted_iota(jnp.int32, (BAND, BAND), 1) + k * BAND, 1.0, 0.0).astype(BF16)
            for k in range(4)
        ]
        onehots.append(jnp.concatenate(parts, axis=1))
    listed = recv_ref[...].reshape(32 * DBLOCKS, 2 * BAND)
    sources = jnp.dot(jnp.concatenate(onehots, axis=0), listed, preferred_element_type=F32).astype(BF16)

    code = code_ref[...]
    cell = lax.broadcasted_iota(jnp.int32, code.shape, 0)
    up = (code * 37) >> 8
    u = (cell >> 4) + up - 3
    v = ((cell & 15) + code - 7 * up + (COLS - 3)) & 15
    source = (u & 7) * COLS + v + jnp.where((u < 0) | (u > 7), CELLS, 0)
    lanes = lax.broadcasted_iota(jnp.int32, (CELLS, 2 * CELLS), 1)
    re = jnp.zeros((CELLS, BAND), F32)
    im = re
    step = 8
    for j0 in range(0, ENTRIES, step):
        picks = [
            jnp.where(source[:, j : j + 1] == lanes, 1.0, 0.0).astype(BF16)
            for j in range(j0, j0 + step)
        ]
        got = jnp.dot(jnp.concatenate(picks, axis=0), sources, preferred_element_type=F32)
        for k in range(step):
            op = chosen_ref[(j0 + k) * CELLS : (j0 + k + 1) * CELLS].astype(F32)
            g = got[k * CELLS : (k + 1) * CELLS]
            gr, gi, wr, wi = g[:, :BAND], g[:, BAND:], op[:, :BAND], op[:, BAND:]
            re = re + (wr * gr - wi * gi)
            im = im + (wr * gi + wi * gr)
    translated = jnp.concatenate([re, im], axis=1).astype(BF16)
    rows = lax.broadcasted_iota(jnp.int32, (CELLS, CELLS), 0)
    onehot = jnp.where(rows == own, 1.0, 0.0).astype(BF16)
    out_ref[...] = jnp.dot(onehot, translated, preferred_element_type=F32).astype(BF16)


def translate(received, packed, code, chosen, order):
    return pl.pallas_call(
        translate_kernel,
        in_specs=[whole()] * 5,
        out_specs=whole(),
        out_shape=jax.ShapeDtypeStruct((CELLS, 2 * BAND), BF16),
        compiler_params=params(),
    )(received, packed, code, chosen, order)


def anterpolate_kernel(recv_ref, interp_ref, cos_ref, sin_ref, out_ref):
    total = jnp.zeros((128, DC), F32)
    rows = 8 * TILE // BAND
    for t in range(TILES):
        at = slice(t * TILE, (t + 1) * TILE)
        c, s = cos_ref[:, at], sin_ref[:, at]
        values = recv_ref[rows * t : rows * (t + 1)].astype(F32)
        blocks = rows // 8
        re = jnp.concatenate([values[8 * d : 8 * d + 8, :BAND] for d in range(blocks)], axis=1)
        im = jnp.concatenate([values[8 * d : 8 * d + 8, BAND:] for d in range(blocks)], axis=1)
        real, imag = [], []
        for k in range(CHILDREN):
            ck, sk = c[k : k + 1], s[k : k + 1]
            real.append(ck * re + sk * im)
            imag.append(ck * im - sk * re)
        shifted = jnp.concatenate(real + imag, axis=0).astype(BF16)
        total += lax.dot_general(
            shifted, interp_ref[:, at], (((1,), (1,)), ((), ())), preferred_element_type=F32
        )
    out_ref[...] = (total * (DC / DP)).astype(BF16)


def anterpolate(received, interp, c, s):
    return pl.pallas_call(
        anterpolate_kernel,
        in_specs=[whole()] * 4,
        out_specs=whole(),
        out_shape=jax.ShapeDtypeStruct((128, DC), BF16),
        compiler_params=params(),
    )(received, interp, c, s)


def outside_pairs(halves, chips):
    pairs = []
    for half in range(halves):
        for chip in range(chips):
            there = half ^ 1 if chip % RUN == RUN - 1 else half
            i = (half * chips + chip) * 2 + 1
            j = (there * chips + (chip + 1) % chips) * 2
            pairs += [(i, j), (j, i)]
    return pairs


def per_device(child_fields, interp_matrix, phase_angle, patch_order, offset_code, operator_index, operators):
    child_rows = child_fields.transpose(2, 1, 0, 3).reshape(128, DC)
    packed = pack(child_rows, patch_order)
    outside = lax.ppermute(packed, ("dir_1", "chip", "core"), outside_pairs(2, lax.axis_size("chip")))
    own, chosen, interp, c, s = front(
        packed,
        operators.reshape(128, 2 * BAND),
        operator_index.reshape(CELLS, ENTRIES),
        interp_matrix,
        phase_angle,
    )
    send = to_send(outside, own, patch_order, interp, c, s)
    listed = lax.all_to_all(send.reshape(2 * DBLOCKS, 16, 2 * BAND), DIR + ("core",), 0, 0, tiled=True)
    returned = translate(
        listed.reshape(DBLOCKS, 2, 16, 2 * BAND), outside, offset_code.reshape(CELLS, ENTRIES), chosen, patch_order
    )
    received = lax.all_to_all(returned.reshape(DBLOCKS, 8, 2 * BAND), DIR, 0, 0, tiled=True)
    fields = anterpolate(received.reshape(8 * DBLOCKS, 2 * BAND), interp, c, s)
    return fields.reshape(2, CHILDREN, 8, DC).transpose(2, 1, 0, 3)


def solution(mesh):
    split = Mesh(mesh.devices.reshape(8, 2, mesh.shape["box"] // 2, 2), ("dir_0", "dir_1", "chip", "core"))
    box = ("chip", "core")
    placed = (
        P(box + DIR, None, None, None),
        P(),
        P(),
        P(box, None),
        P(box, None, None),
        P(box, None, None),
        P(None, None, DIR),
    )
    return jax.shard_map(
        per_device,
        mesh=split,
        in_specs=placed,
        out_specs=P(box + DIR, None, None, None),
        check_vma=False,
    )
```

```python
import jax
import jax.numpy as jnp
from jax import lax
from jax.experimental import pallas as pl
from jax.experimental.pallas import tpu as pltpu
from jax.sharding import Mesh
from jax.sharding import PartitionSpec as P

DC = 512
DP = 2048
CHILDREN = 8
BAND = 128
CELLS = 128
COLS = 16
ENTRIES = 40
DBLOCKS = 16
RUN = 4
TILE = 512
TILES = DP // TILE
DIR = ("dir_0", "dir_1")
F32 = jnp.float32
BF16 = jnp.bfloat16
VMEM_LIMIT = 24 * 1024 * 1024


def params():
    return pltpu.CompilerParams(vmem_limit_bytes=VMEM_LIMIT)


def cos_sin(angle):
    half = angle * 0.5
    sq = half * half
    s = F32(1.0 / 6227020800.0)
    for c in (-1.0 / 39916800.0, 1.0 / 362880.0, -1.0 / 5040.0, 1.0 / 120.0, -1.0 / 6.0, 1.0):
        s = s * sq + F32(c)
    s = s * half
    c_ = F32(1.0 / 479001600.0)
    for c in (-1.0 / 3628800.0, 1.0 / 40320.0, -1.0 / 720.0, 1.0 / 24.0, -0.5, 1.0):
        c_ = c_ * sq + F32(c)
    return 1.0 - 2.0 * s * s, 2.0 * s * c_


def block_fields(child, interp, c, s):
    prod = jnp.dot(child, interp, preferred_element_type=F32)
    re = jnp.zeros((8, prod.shape[1]), F32)
    im = re
    for k in range(CHILDREN):
        pr, pi = prod[8 * k : 8 * k + 8], prod[64 + 8 * k : 72 + 8 * k]
        ck, sk = c[k : k + 1], s[k : k + 1]
        re = re + (ck * pr - sk * pi)
        im = im + (ck * pi + sk * pr)
    columns = [slice(d * BAND, (d + 1) * BAND) for d in range(prod.shape[1] // BAND)]
    return [jnp.concatenate([re[:, at], im[:, at]], axis=1) for at in columns]


def by_part(rows):
    there = lax.broadcasted_iota(jnp.int32, (128, 128), 0)
    here = lax.broadcasted_iota(jnp.int32, (128, 128), 1)
    wanted = (there & 7) * 16 + ((there >> 3) & 7) * 2 + (there >> 6)
    pick = jnp.where(here == wanted, 1.0, 0.0).astype(BF16)
    return jnp.dot(pick, rows, preferred_element_type=F32).astype(BF16)


def by_box(rows):
    there = lax.broadcasted_iota(jnp.int32, (128, 128), 0)
    here = lax.broadcasted_iota(jnp.int32, (128, 128), 1)
    wanted = (there & 1) * 64 + ((there >> 1) & 7) * 8 + (there >> 4)
    pick = jnp.where(here == wanted, 1.0, 0.0).astype(BF16)
    return jnp.dot(pick, rows, preferred_element_type=F32).astype(BF16)


def whole():
    return pl.BlockSpec(memory_space=pltpu.VMEM)


def outer():
    return pl.BlockSpec(memory_space=pltpu.HBM)


def pack_kernel(child_hbm, order_hbm, packed_ref, child_ref, order_ref, sems):
    loads = [
        pltpu.make_async_copy(child_hbm, child_ref, sems.at[0]),
        pltpu.make_async_copy(order_hbm, order_ref, sems.at[1]),
    ]
    for load in loads:
        load.start()
    loads[1].wait()
    order = jnp.broadcast_to(order_ref[...].astype(F32), (16, CELLS)).astype(BF16)
    packed_ref[128:144] = jnp.concatenate([order] * (DC // CELLS), axis=1)
    loads[0].wait()
    packed_ref[:128] = child_ref[...].reshape(128, DC)


def in_hbm(*args):
    return [pltpu.with_memory_space_constraint(x, pltpu.HBM) for x in args]


def pack(child, order):
    return pl.pallas_call(
        pack_kernel,
        in_specs=[outer()] * 2,
        out_specs=whole(),
        out_shape=jax.ShapeDtypeStruct((144, DC), BF16),
        scratch_shapes=[
            pltpu.VMEM((64, 2, DC), BF16),
            pltpu.VMEM((1, CELLS), jnp.int32),
            pltpu.SemaphoreType.DMA((2,)),
        ],
        compiler_params=params(),
    )(*in_hbm(child, order))


def front_kernel(
    packed_ref,
    ops_hbm,
    index_hbm,
    phase_hbm,
    interp_hbm,
    own_ref,
    chosen_ref,
    interp_ref,
    cos_ref,
    sin_ref,
    ops_ref,
    index_ref,
    phase_ref,
    sems,
):
    small = [(ops_hbm, ops_ref), (index_hbm, index_ref), (phase_hbm, phase_ref)]
    loads = [pltpu.make_async_copy(there, here, sems.at[k]) for k, (there, here) in enumerate(small)]
    for t in range(TILES):
        at = pl.ds(t * TILE, TILE)
        loads.append(pltpu.make_async_copy(interp_hbm.at[:, at], interp_ref.at[:, at], sems.at[len(small) + t]))
    for load in loads:
        load.start()
    child = by_part(packed_ref[:128])
    loads[0].wait()
    ops = ops_ref[...].astype(F32)
    ops = jnp.concatenate([ops[:, 0], ops[:, 1]], axis=1).astype(BF16)
    loads[1].wait()
    index = index_ref[...]
    lanes = lax.broadcasted_iota(jnp.int32, (CELLS, BAND), 1)
    step = 8
    for j0 in range(0, ENTRIES, step):
        picks = [
            jnp.where(index[:, j : j + 1] == lanes, 1.0, 0.0).astype(BF16)
            for j in range(j0, j0 + step)
        ]
        chosen = jnp.dot(jnp.concatenate(picks, axis=0), ops, preferred_element_type=F32)
        chosen_ref[j0 * CELLS : (j0 + step) * CELLS] = chosen.astype(BF16)
    loads[2].wait()
    c, s = cos_sin(phase_ref[...])
    cos_ref[...] = c
    sin_ref[...] = s
    for t in range(TILES):
        at = slice(t * TILE, (t + 1) * TILE)
        loads[len(small) + t].wait()
        blocks = block_fields(child, interp_ref[:, at], c[:, at], s[:, at])
        count = 8 * len(blocks)
        own_ref[t * count : (t + 1) * count] = jnp.concatenate(blocks, axis=0).astype(BF16)


def front(packed, *args):
    wave = jax.ShapeDtypeStruct((CHILDREN, DP), F32)
    return pl.pallas_call(
        front_kernel,
        in_specs=[whole()] + [outer()] * 4,
        out_specs=[whole()] * 5,
        out_shape=(
            jax.ShapeDtypeStruct((8 * DBLOCKS, 2 * BAND), BF16),
            jax.ShapeDtypeStruct((ENTRIES * CELLS, 2 * BAND), BF16),
            jax.ShapeDtypeStruct((DC, DP), BF16),
            wave,
            wave,
        ),
        scratch_shapes=[
            pltpu.VMEM((128, 2, BAND), BF16),
            pltpu.VMEM((CELLS, ENTRIES), jnp.int32),
            pltpu.VMEM((CHILDREN, DP), F32),
            pltpu.SemaphoreType.DMA((TILES + 3,)),
        ],
        compiler_params=params(),
        cost_estimate=pl.CostEstimate(flops=4 * 128 * DC * DP, bytes_accessed=DC * DP * 2, transcendentals=0),
    )(packed, *in_hbm(*args))


def send_kernel(packed_ref, own_ref, order_ref, interp_ref, cos_ref, sin_ref, out_ref):
    core = lax.axis_index("core")
    order = order_ref[...].astype(F32)
    order = jnp.broadcast_to(jnp.concatenate([order, order], axis=1), (8, 2 * BAND))
    own = own_ref[...].astype(F32)
    child = by_part(packed_ref[:128])
    for t in range(TILES):
        at = slice(t * TILE, (t + 1) * TILE)
        blocks = block_fields(child, interp_ref[:, at], cos_ref[:, at], sin_ref[:, at])
        for k, block in enumerate(blocks):
            d = t * len(blocks) + k
            first = own[8 * d : 8 * d + 8]
            for c in range(2):
                second = jnp.where(core == c, block, order)
                out_ref[d, c] = jnp.concatenate([first, second], axis=0).astype(BF16)


def to_send(packed, own, order, interp, c, s):
    return pl.pallas_call(
        send_kernel,
        in_specs=[whole()] * 6,
        out_specs=whole(),
        out_shape=jax.ShapeDtypeStruct((DBLOCKS, 2, 16, 2 * BAND), BF16),
        compiler_params=params(),
        cost_estimate=pl.CostEstimate(flops=2 * 128 * DC * DP, bytes_accessed=DC * DP * 2, transcendentals=0),
    )(packed, own, order, interp, c, s)


def translate_kernel(recv_ref, packed_ref, code_ref, chosen_ref, order_ref, out_ref):
    core, chip = lax.axis_index("core"), lax.axis_index("chip")
    flip = jnp.where(core == 0, jnp.where(chip % RUN == 0, 8, 0), jnp.where(chip % RUN == RUN - 1, 8, 0))
    own = order_ref[...]
    mates = [recv_ref[0, c].astype(F32)[8:9, :BAND] for c in range(2)]
    mate = jnp.where(core == 0, mates[1], mates[0]).astype(jnp.int32)
    outside = packed_ref[128:144].astype(F32)[0:1, :BAND].astype(jnp.int32)

    def row_of(position, c, half):
        return (position >> 3) * 32 + c * 16 + half * 8 + (position & 7)

    inside_row = row_of(own, core, 0)
    mate_row = row_of(mate, 1 - core, 0)
    outside_row = row_of(outside ^ flip, core, 1)
    lane = lax.broadcasted_iota(jnp.int32, (1, BAND), 1)
    edge_row = jnp.where((lane < 64) == (core == 0), mate_row, outside_row)
    onehots = []
    for rows in (inside_row, edge_row):
        column = jnp.broadcast_to(rows.astype(F32), (BAND, BAND)).T.astype(jnp.int32)
        parts = [
            jnp.where(column == lax.broadcasted_iota(jnp.int32, (BAND, BAND), 1) + k * BAND, 1.0, 0.0).astype(BF16)
            for k in range(4)
        ]
        onehots.append(jnp.concatenate(parts, axis=1))
    listed = recv_ref[...].reshape(32 * DBLOCKS, 2 * BAND)
    sources = jnp.dot(jnp.concatenate(onehots, axis=0), listed, preferred_element_type=F32).astype(BF16)

    code = code_ref[...]
    cell = lax.broadcasted_iota(jnp.int32, code.shape, 0)
    up = (code * 37) >> 8
    u = (cell >> 4) + up - 3
    v = ((cell & 15) + code - 7 * up + (COLS - 3)) & 15
    source = (u & 7) * COLS + v + jnp.where((u < 0) | (u > 7), CELLS, 0)
    lanes = lax.broadcasted_iota(jnp.int32, (CELLS, 2 * CELLS), 1)
    re = jnp.zeros((CELLS, BAND), F32)
    im = re
    step = 8
    for j0 in range(0, ENTRIES, step):
        picks = [
            jnp.where(source[:, j : j + 1] == lanes, 1.0, 0.0).astype(BF16)
            for j in range(j0, j0 + step)
        ]
        got = jnp.dot(jnp.concatenate(picks, axis=0), sources, preferred_element_type=F32)
        for k in range(step):
            op = chosen_ref[(j0 + k) * CELLS : (j0 + k + 1) * CELLS].astype(F32)
            g = got[k * CELLS : (k + 1) * CELLS]
            gr, gi, wr, wi = g[:, :BAND], g[:, BAND:], op[:, :BAND], op[:, BAND:]
            re = re + (wr * gr - wi * gi)
            im = im + (wr * gi + wi * gr)
    translated = jnp.concatenate([re, im], axis=1).astype(BF16)
    rows = lax.broadcasted_iota(jnp.int32, (CELLS, CELLS), 0)
    onehot = jnp.where(rows == own, 1.0, 0.0).astype(BF16)
    out_ref[...] = jnp.dot(onehot, translated, preferred_element_type=F32).astype(BF16)


def translate(received, packed, code, chosen, order):
    return pl.pallas_call(
        translate_kernel,
        in_specs=[whole()] * 5,
        out_specs=whole(),
        out_shape=jax.ShapeDtypeStruct((CELLS, 2 * BAND), BF16),
        compiler_params=params(),
    )(received, packed, code, chosen, order)


def anterpolate_kernel(recv_ref, interp_ref, cos_ref, sin_ref, out_ref):
    total = jnp.zeros((128, DC), F32)
    rows = 8 * TILE // BAND
    for t in range(TILES):
        at = slice(t * TILE, (t + 1) * TILE)
        c, s = cos_ref[:, at], sin_ref[:, at]
        values = recv_ref[rows * t : rows * (t + 1)].astype(F32)
        blocks = rows // 8
        re = jnp.concatenate([values[8 * d : 8 * d + 8, :BAND] for d in range(blocks)], axis=1)
        im = jnp.concatenate([values[8 * d : 8 * d + 8, BAND:] for d in range(blocks)], axis=1)
        real, imag = [], []
        for k in range(CHILDREN):
            ck, sk = c[k : k + 1], s[k : k + 1]
            real.append(ck * re + sk * im)
            imag.append(ck * im - sk * re)
        shifted = jnp.concatenate(real + imag, axis=0).astype(BF16)
        total += lax.dot_general(
            shifted, interp_ref[:, at], (((1,), (1,)), ((), ())), preferred_element_type=F32
        )
    rows = by_box((total * (DC / DP)).astype(BF16))
    out_ref[...] = rows.reshape(64, 2, DC)


def anterpolate(received, interp, c, s):
    return pl.pallas_call(
        anterpolate_kernel,
        in_specs=[whole()] * 4,
        out_specs=whole(),
        out_shape=jax.ShapeDtypeStruct((64, 2, DC), BF16),
        compiler_params=params(),
    )(received, interp, c, s)


def outside_pairs(halves, chips):
    pairs = []
    for half in range(halves):
        for chip in range(chips):
            there = half ^ 1 if chip % RUN == RUN - 1 else half
            i = (half * chips + chip) * 2 + 1
            j = (there * chips + (chip + 1) % chips) * 2
            pairs += [(i, j), (j, i)]
    return pairs


def per_device(child_fields, interp_matrix, phase_angle, patch_order, offset_code, operator_index, operators):
    packed = pack(child_fields.reshape(64, 2, DC), patch_order)
    outside = lax.ppermute(packed, ("dir_1", "chip", "core"), outside_pairs(2, lax.axis_size("chip")))
    own, chosen, interp, c, s = front(
        packed, operators, operator_index.reshape(CELLS, ENTRIES), phase_angle, interp_matrix
    )
    send = to_send(outside, own, patch_order, interp, c, s)
    listed = lax.all_to_all(send.reshape(2 * DBLOCKS, 16, 2 * BAND), DIR + ("core",), 0, 0, tiled=True)
    returned = translate(
        listed.reshape(DBLOCKS, 2, 16, 2 * BAND), outside, offset_code.reshape(CELLS, ENTRIES), chosen, patch_order
    )
    received = lax.all_to_all(returned.reshape(DBLOCKS, 8, 2 * BAND), DIR, 0, 0, tiled=True)
    fields = anterpolate(received.reshape(8 * DBLOCKS, 2 * BAND), interp, c, s)
    return fields.reshape(8, CHILDREN, 2, DC)


def solution(mesh):
    split = Mesh(mesh.devices.reshape(8, 2, mesh.shape["box"] // 2, 2), ("dir_0", "dir_1", "chip", "core"))
    box = ("chip", "core")
    placed = (
        P(box + DIR, None, None, None),
        P(),
        P(),
        P(box, None),
        P(box, None, None),
        P(box, None, None),
        P(None, None, DIR),
    )
    return jax.shard_map(
        per_device,
        mesh=split,
        in_specs=placed,
        out_specs=P(box + DIR, None, None, None),
        check_vma=False,
    )
```

```python
import jax
import jax.numpy as jnp
from jax import lax
from jax.experimental import pallas as pl
from jax.experimental.pallas import tpu as pltpu
from jax.sharding import Mesh
from jax.sharding import PartitionSpec as P

DC = 512
DP = 2048
CHILDREN = 8
BAND = 128
CELLS = 128
COLS = 16
ENTRIES = 40
DBLOCKS = 16
HALO = 48
TILE = 512
TILES = DP // TILE
DIR = ("dir_0", "dir_1")
F32 = jnp.float32
BF16 = jnp.bfloat16
VMEM_LIMIT = 24 * 1024 * 1024


def params():
    return pltpu.CompilerParams(vmem_limit_bytes=VMEM_LIMIT)


def cos_sin(angle):
    half = angle * 0.5
    sq = half * half
    s = F32(1.0 / 6227020800.0)
    for c in (-1.0 / 39916800.0, 1.0 / 362880.0, -1.0 / 5040.0, 1.0 / 120.0, -1.0 / 6.0, 1.0):
        s = s * sq + F32(c)
    s = s * half
    c_ = F32(1.0 / 479001600.0)
    for c in (-1.0 / 3628800.0, 1.0 / 40320.0, -1.0 / 720.0, 1.0 / 24.0, -0.5, 1.0):
        c_ = c_ * sq + F32(c)
    return 1.0 - 2.0 * s * s, 2.0 * s * c_


def block_fields(child, interp, c, s):
    prod = jnp.dot(child, interp, preferred_element_type=F32)
    re = jnp.zeros((8, prod.shape[1]), F32)
    im = re
    for k in range(CHILDREN):
        pr, pi = prod[8 * k : 8 * k + 8], prod[64 + 8 * k : 72 + 8 * k]
        ck, sk = c[k : k + 1], s[k : k + 1]
        re = re + (ck * pr - sk * pi)
        im = im + (ck * pi + sk * pr)
    columns = [slice(d * BAND, (d + 1) * BAND) for d in range(prod.shape[1] // BAND)]
    return [jnp.concatenate([re[:, at], im[:, at]], axis=1) for at in columns]


def by_part(rows):
    there = lax.broadcasted_iota(jnp.int32, (128, 128), 0)
    here = lax.broadcasted_iota(jnp.int32, (128, 128), 1)
    wanted = (there & 7) * 16 + ((there >> 3) & 7) * 2 + (there >> 6)
    pick = jnp.where(here == wanted, 1.0, 0.0).astype(BF16)
    return jnp.dot(pick, rows, preferred_element_type=F32).astype(BF16)


def by_box(rows):
    there = lax.broadcasted_iota(jnp.int32, (128, 128), 0)
    here = lax.broadcasted_iota(jnp.int32, (128, 128), 1)
    wanted = (there & 1) * 64 + ((there >> 1) & 7) * 8 + (there >> 4)
    pick = jnp.where(here == wanted, 1.0, 0.0).astype(BF16)
    return jnp.dot(pick, rows, preferred_element_type=F32).astype(BF16)


def whole():
    return pl.BlockSpec(memory_space=pltpu.VMEM)


def outer():
    return pl.BlockSpec(memory_space=pltpu.HBM)


def in_hbm(*args):
    return [pltpu.with_memory_space_constraint(x, pltpu.HBM) for x in args]


def front_kernel(
    child_hbm, order_hbm, phase_hbm, interp_hbm, send_ref, interp_ref, cos_ref, sin_ref, child_ref, order_ref, phase_ref, sems
):
    small = [(child_hbm, child_ref), (order_hbm, order_ref), (phase_hbm, phase_ref)]
    loads = [pltpu.make_async_copy(there, here, sems.at[k]) for k, (there, here) in enumerate(small)]
    for t in range(TILES):
        at = pl.ds(t * TILE, TILE)
        loads.append(pltpu.make_async_copy(interp_hbm.at[:, at], interp_ref.at[:, at], sems.at[len(small) + t]))
    for load in loads:
        load.start()
    loads[0].wait()
    child = by_part(child_ref[...].reshape(128, DC))
    loads[1].wait()
    order = jnp.broadcast_to(order_ref[...].astype(F32), (8, CELLS))
    loads[2].wait()
    c, s = cos_sin(phase_ref[...])
    cos_ref[...] = c
    sin_ref[...] = s
    for t in range(TILES):
        at = slice(t * TILE, (t + 1) * TILE)
        loads[len(small) + t].wait()
        blocks = block_fields(child, interp_ref[:, at], c[:, at], s[:, at])
        for k, block in enumerate(blocks):
            d = t * len(blocks) + k
            out = jnp.concatenate([block, order], axis=1).astype(BF16)
            send_ref[2 * d] = out
            send_ref[2 * d + 1] = out


def front(*args):
    wave = jax.ShapeDtypeStruct((CHILDREN, DP), F32)
    return pl.pallas_call(
        front_kernel,
        in_specs=[outer()] * 4,
        out_specs=[whole()] * 4,
        out_shape=(
            jax.ShapeDtypeStruct((2 * DBLOCKS, 8, 3 * BAND), BF16),
            jax.ShapeDtypeStruct((DC, DP), BF16),
            wave,
            wave,
        ),
        scratch_shapes=[
            pltpu.VMEM((64, 2, DC), BF16),
            pltpu.VMEM((1, CELLS), jnp.int32),
            pltpu.VMEM((CHILDREN, DP), F32),
            pltpu.SemaphoreType.DMA((TILES + 3,)),
        ],
        compiler_params=params(),
        cost_estimate=pl.CostEstimate(flops=2 * 128 * DC * DP, bytes_accessed=DC * DP * 2, transcendentals=0),
    )(*in_hbm(*args))


def cells_kernel(recv_ref, order_ref, sources_ref, edge_ref):
    core = lax.axis_index("core")
    own = order_ref[...]
    ends = recv_ref[:16, 2 * BAND :].astype(F32)
    mate = jnp.where(core == 0, ends[0:1], ends[8:9]).astype(jnp.int32)
    onehots = []
    for position, side in ((own, 1 - core), (mate, core)):
        rows = (position >> 3) * 16 + side * 8 + (position & 7)
        column = jnp.broadcast_to(rows.astype(F32), (BAND, BAND)).T.astype(jnp.int32)
        parts = [
            jnp.where(column == lax.broadcasted_iota(jnp.int32, (BAND, BAND), 1) + k * BAND, 1.0, 0.0).astype(BF16)
            for k in range(2)
        ]
        onehots.append(jnp.concatenate(parts, axis=1))
    listed = recv_ref[:, : 2 * BAND]
    sources = jnp.dot(jnp.concatenate(onehots, axis=0), listed, preferred_element_type=F32)
    sources_ref[...] = sources.astype(BF16)
    edge_ref[...] = jnp.where(core == 0, sources[CELLS - HALO : CELLS], sources[:HALO]).astype(BF16)


def to_cells(received, order):
    return pl.pallas_call(
        cells_kernel,
        in_specs=[whole()] * 2,
        out_specs=[whole()] * 2,
        out_shape=(
            jax.ShapeDtypeStruct((2 * CELLS, 2 * BAND), BF16),
            jax.ShapeDtypeStruct((HALO, 2 * BAND), BF16),
        ),
        compiler_params=params(),
    )(received, order)


def operators_kernel(index_ref, ops_ref, out_ref):
    ops = ops_ref[...].astype(F32)
    ops = jnp.concatenate([ops[:, 0], ops[:, 1]], axis=1).astype(BF16)
    index = index_ref[...]
    lanes = lax.broadcasted_iota(jnp.int32, (CELLS, BAND), 1)
    step = 8
    for j0 in range(0, ENTRIES, step):
        picks = [
            jnp.where(index[:, j : j + 1] == lanes, 1.0, 0.0).astype(BF16)
            for j in range(j0, j0 + step)
        ]
        chosen = jnp.dot(jnp.concatenate(picks, axis=0), ops, preferred_element_type=F32)
        out_ref[j0 * CELLS : (j0 + step) * CELLS] = chosen.astype(BF16)


def chosen_operators(index, ops):
    return pl.pallas_call(
        operators_kernel,
        in_specs=[whole()] * 2,
        out_specs=whole(),
        out_shape=jax.ShapeDtypeStruct((ENTRIES * CELLS, 2 * BAND), BF16),
        compiler_params=params(),
        cost_estimate=pl.CostEstimate(
            flops=2 * ENTRIES * CELLS * 128 * 256, bytes_accessed=ENTRIES * CELLS * 512, transcendentals=0
        ),
    )(index, ops)


def translate_kernel(sources_ref, edge_ref, code_ref, chosen_ref, order_ref, out_ref):
    core = lax.axis_index("core")
    edge = edge_ref[...].astype(F32)
    outside = sources_ref[CELLS:].astype(F32)
    first = jnp.concatenate([edge, outside[HALO:]], axis=0)
    second = jnp.concatenate([outside[: CELLS - HALO], edge], axis=0)
    edges = jnp.where(core == 0, first, second).astype(BF16)
    sources = jnp.concatenate([sources_ref[:CELLS], edges], axis=0)

    code = code_ref[...]
    cell = lax.broadcasted_iota(jnp.int32, code.shape, 0)
    up = (code * 37) >> 8
    u = (cell >> 4) + up - 3
    v = ((cell & 15) + code - 7 * up + (COLS - 3)) & 15
    source = (u & 7) * COLS + v + jnp.where((u < 0) | (u > 7), CELLS, 0)
    lanes = lax.broadcasted_iota(jnp.int32, (CELLS, 2 * CELLS), 1)
    re = jnp.zeros((CELLS, BAND), F32)
    im = re
    step = 8
    for j0 in range(0, ENTRIES, step):
        picks = [
            jnp.where(source[:, j : j + 1] == lanes, 1.0, 0.0).astype(BF16)
            for j in range(j0, j0 + step)
        ]
        got = jnp.dot(jnp.concatenate(picks, axis=0), sources, preferred_element_type=F32)
        for k in range(step):
            op = chosen_ref[(j0 + k) * CELLS : (j0 + k + 1) * CELLS].astype(F32)
            g = got[k * CELLS : (k + 1) * CELLS]
            gr, gi, wr, wi = g[:, :BAND], g[:, BAND:], op[:, :BAND], op[:, BAND:]
            re = re + (wr * gr - wi * gi)
            im = im + (wr * gi + wi * gr)
    translated = jnp.concatenate([re, im], axis=1).astype(BF16)
    rows = lax.broadcasted_iota(jnp.int32, (CELLS, CELLS), 0)
    onehot = jnp.where(rows == order_ref[...], 1.0, 0.0).astype(BF16)
    out_ref[...] = jnp.dot(onehot, translated, preferred_element_type=F32).astype(BF16)


def translate(sources, edge, code, chosen, order):
    return pl.pallas_call(
        translate_kernel,
        in_specs=[whole()] * 5,
        out_specs=whole(),
        out_shape=jax.ShapeDtypeStruct((CELLS, 2 * BAND), BF16),
        compiler_params=params(),
    )(sources, edge, code, chosen, order)


def anterpolate_kernel(recv_ref, interp_ref, cos_ref, sin_ref, out_ref):
    total = jnp.zeros((128, DC), F32)
    rows = 8 * TILE // BAND
    for t in range(TILES):
        at = slice(t * TILE, (t + 1) * TILE)
        c, s = cos_ref[:, at], sin_ref[:, at]
        values = recv_ref[rows * t : rows * (t + 1)].astype(F32)
        blocks = rows // 8
        re = jnp.concatenate([values[8 * d : 8 * d + 8, :BAND] for d in range(blocks)], axis=1)
        im = jnp.concatenate([values[8 * d : 8 * d + 8, BAND:] for d in range(blocks)], axis=1)
        real, imag = [], []
        for k in range(CHILDREN):
            ck, sk = c[k : k + 1], s[k : k + 1]
            real.append(ck * re + sk * im)
            imag.append(ck * im - sk * re)
        shifted = jnp.concatenate(real + imag, axis=0).astype(BF16)
        total += lax.dot_general(
            shifted, interp_ref[:, at], (((1,), (1,)), ((), ())), preferred_element_type=F32
        )
    rows = by_box((total * (DC / DP)).astype(BF16))
    out_ref[...] = rows.reshape(64, 2, DC)


def anterpolate(received, interp, c, s):
    return pl.pallas_call(
        anterpolate_kernel,
        in_specs=[whole()] * 4,
        out_specs=whole(),
        out_shape=jax.ShapeDtypeStruct((64, 2, DC), BF16),
        compiler_params=params(),
    )(received, interp, c, s)


def neighbour_groups(chips):
    groups = []
    for chip in range(chips):
        sides = (2 * chip + 1, 2 * ((chip + 1) % chips))
        groups.append([d * 2 * chips + side for d in range(DBLOCKS) for side in sides])
    return groups


def per_device(child_fields, interp_matrix, phase_angle, patch_order, offset_code, operator_index, operators):
    send, interp, c, s = front(child_fields.reshape(64, 2, DC), patch_order, phase_angle, interp_matrix)
    received = lax.all_to_all(
        send, DIR + ("chip", "core"), 0, 0, axis_index_groups=neighbour_groups(lax.axis_size("chip")), tiled=True
    )
    sources, edge = to_cells(received.reshape(256, 3 * BAND), patch_order)
    index, edge = lax.optimization_barrier((operator_index.reshape(CELLS, ENTRIES), edge))
    chosen = chosen_operators(index, operators)
    edge = lax.ppermute(edge, "core", [(0, 1), (1, 0)])
    returned = translate(sources, edge, offset_code.reshape(CELLS, ENTRIES), chosen, patch_order)
    back = lax.all_to_all(returned.reshape(DBLOCKS, 8, 2 * BAND), DIR, 0, 0, tiled=True)
    fields = anterpolate(back.reshape(8 * DBLOCKS, 2 * BAND), interp, c, s)
    return fields.reshape(8, CHILDREN, 2, DC)


def solution(mesh):
    split = Mesh(mesh.devices.reshape(8, 2, mesh.shape["box"] // 2, 2), ("dir_0", "dir_1", "chip", "core"))
    box = ("chip", "core")
    placed = (
        P(box + DIR, None, None, None),
        P(),
        P(),
        P(box, None),
        P(box, None, None),
        P(box, None, None),
        P(None, None, DIR),
    )
    return jax.shard_map(
        per_device,
        mesh=split,
        in_specs=placed,
        out_specs=P(box + DIR, None, None, None),
        check_vma=False,
    )
```

```python
import jax
import jax.numpy as jnp
from jax import lax
from jax.experimental import pallas as pl
from jax.experimental.pallas import tpu as pltpu
from jax.sharding import Mesh
from jax.sharding import PartitionSpec as P

DC = 512
DP = 2048
CHILDREN = 8
BAND = 128
CELLS = 128
COLS = 16
ENTRIES = 40
DBLOCKS = 16
HALO = 48
WIDE = 4 * BAND
RUN = 4
TILE = 512
TILES = DP // TILE
DIR = ("dir_0", "dir_1")
F32 = jnp.float32
BF16 = jnp.bfloat16
VMEM_LIMIT = 24 * 1024 * 1024


def params():
    return pltpu.CompilerParams(vmem_limit_bytes=VMEM_LIMIT)


def cos_sin(angle):
    half = angle * 0.5
    sq = half * half
    s = F32(1.0 / 6227020800.0)
    for c in (-1.0 / 39916800.0, 1.0 / 362880.0, -1.0 / 5040.0, 1.0 / 120.0, -1.0 / 6.0, 1.0):
        s = s * sq + F32(c)
    s = s * half
    c_ = F32(1.0 / 479001600.0)
    for c in (-1.0 / 3628800.0, 1.0 / 40320.0, -1.0 / 720.0, 1.0 / 24.0, -0.5, 1.0):
        c_ = c_ * sq + F32(c)
    return 1.0 - 2.0 * s * s, 2.0 * s * c_


def block_fields(child, interp, c, s):
    prod = jnp.dot(child, interp, preferred_element_type=F32)
    re = jnp.zeros((8, prod.shape[1]), F32)
    im = re
    for k in range(CHILDREN):
        pr, pi = prod[8 * k : 8 * k + 8], prod[64 + 8 * k : 72 + 8 * k]
        ck, sk = c[k : k + 1], s[k : k + 1]
        re = re + (ck * pr - sk * pi)
        im = im + (ck * pi + sk * pr)
    columns = [slice(d * BAND, (d + 1) * BAND) for d in range(prod.shape[1] // BAND)]
    return [jnp.concatenate([re[:, at], im[:, at]], axis=1) for at in columns]


def by_part(rows):
    there = lax.broadcasted_iota(jnp.int32, (128, 128), 0)
    here = lax.broadcasted_iota(jnp.int32, (128, 128), 1)
    wanted = (there & 7) * 16 + ((there >> 3) & 7) * 2 + (there >> 6)
    pick = jnp.where(here == wanted, 1.0, 0.0).astype(BF16)
    return jnp.dot(pick, rows, preferred_element_type=F32).astype(BF16)


def by_box(rows):
    there = lax.broadcasted_iota(jnp.int32, (128, 128), 0)
    here = lax.broadcasted_iota(jnp.int32, (128, 128), 1)
    wanted = (there & 1) * 64 + ((there >> 1) & 7) * 8 + (there >> 4)
    pick = jnp.where(here == wanted, 1.0, 0.0).astype(BF16)
    return jnp.dot(pick, rows, preferred_element_type=F32).astype(BF16)


def whole():
    return pl.BlockSpec(memory_space=pltpu.VMEM)


def outer():
    return pl.BlockSpec(memory_space=pltpu.HBM)


def in_hbm(*args):
    return [pltpu.with_memory_space_constraint(x, pltpu.HBM) for x in args]


def front_kernel(
    child_hbm, order_hbm, phase_hbm, interp_hbm, send_ref, cos_ref, sin_ref, child_ref, order_ref, phase_ref, interp_ref, sems
):
    small = [(child_hbm, child_ref), (order_hbm, order_ref), (phase_hbm, phase_ref)]
    loads = [pltpu.make_async_copy(there, here, sems.at[k]) for k, (there, here) in enumerate(small)]
    for t in range(TILES):
        at = pl.ds(t * TILE, TILE)
        loads.append(pltpu.make_async_copy(interp_hbm.at[:, at], interp_ref.at[:, at], sems.at[len(small) + t]))
    for load in loads:
        load.start()
    loads[0].wait()
    child = by_part(child_ref[...].reshape(128, DC))
    loads[1].wait()
    order = jnp.broadcast_to(order_ref[...].astype(F32), (8, CELLS))
    loads[2].wait()
    c, s = cos_sin(phase_ref[...])
    cos_ref[...] = c
    sin_ref[...] = s
    for t in range(TILES):
        at = slice(t * TILE, (t + 1) * TILE)
        loads[len(small) + t].wait()
        blocks = block_fields(child, interp_ref[:, at], c[:, at], s[:, at])
        for k in range(0, len(blocks), 2):
            at = t * len(blocks) + k
            out = jnp.concatenate([blocks[k], blocks[k + 1], order], axis=1).astype(BF16)
            send_ref[at] = out
            send_ref[at + 1] = out


def front(*args):
    wave = jax.ShapeDtypeStruct((CHILDREN, DP), F32)
    return pl.pallas_call(
        front_kernel,
        in_specs=[outer()] * 4,
        out_specs=[whole()] * 3,
        out_shape=(
            jax.ShapeDtypeStruct((DBLOCKS, 8, WIDE + BAND), BF16),
            wave,
            wave,
        ),
        scratch_shapes=[
            pltpu.VMEM((64, 2, DC), BF16),
            pltpu.VMEM((1, CELLS), jnp.int32),
            pltpu.VMEM((CHILDREN, DP), F32),
            pltpu.VMEM((DC, DP), BF16),
            pltpu.SemaphoreType.DMA((TILES + 3,)),
        ],
        compiler_params=params(),
        cost_estimate=pl.CostEstimate(flops=2 * 128 * DC * DP, bytes_accessed=DC * DP * 2, transcendentals=0),
    )(*in_hbm(*args))


def cells_kernel(recv_ref, order_ref, done_ref, sources_ref, edge_ref):
    core, half, chip = lax.axis_index("core"), lax.axis_index("dir_1"), lax.axis_index("chip")
    turned = jnp.where(core == 0, chip % RUN == 0, chip % RUN == RUN - 1).astype(jnp.int32)
    own = order_ref[...]
    ends = recv_ref[:16, WIDE:].astype(F32)
    mate = jnp.where(core == 0, ends[0:1], ends[8:9]).astype(jnp.int32)
    onehots = []
    for position, side, held in ((own, 1 - core, half), (mate, core, half ^ turned)):
        rows = (position >> 4) * 16 + side * 8 + (position & 7)
        rows = jnp.where(((position >> 3) & 1) == held, rows, -1)
        column = jnp.broadcast_to(rows.astype(F32), (BAND, BAND)).T.astype(jnp.int32)
        lanes = lax.broadcasted_iota(jnp.int32, (BAND, BAND), 1)
        onehots.append(jnp.where(column == lanes, 1.0, 0.0).astype(BF16))
    sources = jnp.dot(jnp.concatenate(onehots, axis=0), recv_ref[:, :WIDE], preferred_element_type=F32)
    sources_ref[...] = sources.astype(BF16)
    edge_ref[...] = jnp.where(core == 0, sources[CELLS - HALO : CELLS], sources[:HALO]).astype(BF16)


def to_cells(received, order, done):
    return pl.pallas_call(
        cells_kernel,
        in_specs=[whole()] * 3,
        out_specs=[whole()] * 2,
        out_shape=(
            jax.ShapeDtypeStruct((2 * CELLS, WIDE), BF16),
            jax.ShapeDtypeStruct((HALO, WIDE), BF16),
        ),
        compiler_params=params(),
    )(received, order, done)


def choose(index, ops, out_ref):
    ops = ops.astype(F32)
    ops = jnp.concatenate([ops[:, 0], ops[:, 1]], axis=1).astype(BF16)
    lanes = lax.broadcasted_iota(jnp.int32, (CELLS, BAND), 1)
    step = 8
    for j0 in range(0, ENTRIES, step):
        picks = [
            jnp.where(index[:, j : j + 1] == lanes, 1.0, 0.0).astype(BF16)
            for j in range(j0, j0 + step)
        ]
        chosen = jnp.dot(jnp.concatenate(picks, axis=0), ops, preferred_element_type=F32)
        out_ref[j0 * CELLS : (j0 + step) * CELLS] = chosen.astype(BF16)


def own_operators_kernel(index_hbm, ops_hbm, out_ref, done_ref, index_ref, ops_ref, sems):
    loads = [
        pltpu.make_async_copy(index_hbm, index_ref, sems.at[0]),
        pltpu.make_async_copy(ops_hbm, ops_ref, sems.at[1]),
    ]
    for load in loads:
        load.start()
    for load in loads:
        load.wait()
    choose(index_ref[...], ops_ref[...], out_ref)
    done_ref[...] = jnp.zeros_like(done_ref)


def other_operators_kernel(index_ref, ops_ref, out_ref):
    choose(index_ref[...], ops_ref[...], out_ref)


CHOICE = pl.CostEstimate(flops=2 * ENTRIES * CELLS * 128 * 256, bytes_accessed=ENTRIES * CELLS * 512, transcendentals=0)


def own_operators(index, ops):
    return pl.pallas_call(
        own_operators_kernel,
        in_specs=[outer()] * 2,
        out_specs=[whole()] * 2,
        out_shape=(
            jax.ShapeDtypeStruct((ENTRIES * CELLS, 2 * BAND), BF16),
            jax.ShapeDtypeStruct((8, BAND), F32),
        ),
        scratch_shapes=[
            pltpu.VMEM((CELLS, ENTRIES), jnp.int32),
            pltpu.VMEM((128, 2, BAND), BF16),
            pltpu.SemaphoreType.DMA((2,)),
        ],
        compiler_params=params(),
        cost_estimate=CHOICE,
    )(*in_hbm(index, ops))


def other_operators(index, ops):
    return pl.pallas_call(
        other_operators_kernel,
        in_specs=[whole()] * 2,
        out_specs=whole(),
        out_shape=jax.ShapeDtypeStruct((ENTRIES * CELLS, 2 * BAND), BF16),
        compiler_params=params(),
        cost_estimate=CHOICE,
    )(index, ops)


def translate_kernel(sources_ref, edge_ref, code_ref, own_ref, other_ref, order_ref, out_ref):
    core, half = lax.axis_index("core"), lax.axis_index("dir_1")
    edge = edge_ref[...].astype(F32)
    outside = sources_ref[CELLS:].astype(F32)
    first = jnp.concatenate([edge, outside[HALO:]], axis=0)
    second = jnp.concatenate([outside[: CELLS - HALO], edge], axis=0)
    edges = jnp.where(core == 0, first, second).astype(BF16)
    sources = jnp.concatenate([sources_ref[:CELLS], edges], axis=0)
    low, high = sources[:, : 2 * BAND], sources[:, 2 * BAND :]
    sides = ((jnp.where(half == 0, low, high), own_ref), (jnp.where(half == 0, high, low), other_ref))

    code = code_ref[...]
    cell = lax.broadcasted_iota(jnp.int32, code.shape, 0)
    up = (code * 37) >> 8
    u = (cell >> 4) + up - 3
    v = ((cell & 15) + code - 7 * up + (COLS - 3)) & 15
    source = (u & 7) * COLS + v + jnp.where((u < 0) | (u > 7), CELLS, 0)
    lanes = lax.broadcasted_iota(jnp.int32, (CELLS, 2 * CELLS), 1)
    totals = [jnp.zeros((CELLS, BAND), F32)] * 4
    step = 8
    for j0 in range(0, ENTRIES, step):
        picks = [
            jnp.where(source[:, j : j + 1] == lanes, 1.0, 0.0).astype(BF16)
            for j in range(j0, j0 + step)
        ]
        picks = jnp.concatenate(picks, axis=0)
        for h, (fields, chosen_ref) in enumerate(sides):
            got = jnp.dot(picks, fields, preferred_element_type=F32)
            re, im = totals[2 * h : 2 * h + 2]
            for k in range(step):
                op = chosen_ref[(j0 + k) * CELLS : (j0 + k + 1) * CELLS].astype(F32)
                g = got[k * CELLS : (k + 1) * CELLS]
                gr, gi, wr, wi = g[:, :BAND], g[:, BAND:], op[:, :BAND], op[:, BAND:]
                re = re + (wr * gr - wi * gi)
                im = im + (wr * gi + wi * gr)
            totals[2 * h : 2 * h + 2] = re, im
    own, other = jnp.concatenate(totals[:2], axis=1), jnp.concatenate(totals[2:], axis=1)
    translated = jnp.concatenate([jnp.where(half == 0, own, other), jnp.where(half == 0, other, own)], axis=1).astype(BF16)
    rows = lax.broadcasted_iota(jnp.int32, (CELLS, CELLS), 0)
    onehot = jnp.where(rows == order_ref[...], 1.0, 0.0).astype(BF16)
    out_ref[...] = jnp.dot(onehot, translated, preferred_element_type=F32).astype(BF16)


def translate(*args):
    return pl.pallas_call(
        translate_kernel,
        in_specs=[whole()] * 6,
        out_specs=whole(),
        out_shape=jax.ShapeDtypeStruct((CELLS, WIDE), BF16),
        compiler_params=params(),
    )(*args)


def anterpolate_kernel(recv_ref, interp_ref, cos_ref, sin_ref, out_ref):
    total = jnp.zeros((128, DC), F32)
    per_tile = TILE // (2 * BAND)
    for t in range(TILES):
        at = slice(t * TILE, (t + 1) * TILE)
        c, s = cos_ref[:, at], sin_ref[:, at]
        values = recv_ref[16 * per_tile * t : 16 * per_tile * (t + 1)].astype(F32)
        re, im = [], []
        for y in range(per_tile):
            both = values[16 * y : 16 * y + 8] + values[16 * y + 8 : 16 * y + 16]
            re += [both[:, :BAND], both[:, 2 * BAND : 3 * BAND]]
            im += [both[:, BAND : 2 * BAND], both[:, 3 * BAND :]]
        re, im = jnp.concatenate(re, axis=1), jnp.concatenate(im, axis=1)
        real, imag = [], []
        for k in range(CHILDREN):
            ck, sk = c[k : k + 1], s[k : k + 1]
            real.append(ck * re + sk * im)
            imag.append(ck * im - sk * re)
        shifted = jnp.concatenate(real + imag, axis=0).astype(BF16)
        total += lax.dot_general(
            shifted, interp_ref[:, at], (((1,), (1,)), ((), ())), preferred_element_type=F32
        )
    rows = by_box((total * (DC / DP)).astype(BF16))
    out_ref[...] = rows.reshape(64, 2, DC)


def anterpolate(received, interp, c, s):
    return pl.pallas_call(
        anterpolate_kernel,
        in_specs=[whole()] * 4,
        out_specs=whole(),
        out_shape=jax.ShapeDtypeStruct((64, 2, DC), BF16),
        compiler_params=params(),
    )(received, interp, c, s)


def neighbour_groups(chips):
    groups = []
    for half in range(2):
        for chip in range(chips):
            there = half ^ 1 if chip % RUN == RUN - 1 else half
            sides = ((half * chips + chip) * 2 + 1, (there * chips + (chip + 1) % chips) * 2)
            groups.append([y * 4 * chips + side for y in range(DBLOCKS // 2) for side in sides])
    return groups


def other_half(chips):
    pairs = []
    for half in range(2):
        for chip in range(chips):
            for core in range(2):
                pairs.append(((half * chips + chip) * 2 + core, ((half ^ 1) * chips + (chip ^ 2)) * 2 + core))
    return pairs


def per_device(child_fields, interp_matrix, phase_angle, patch_order, offset_code, operator_index, operators):
    chips = lax.axis_size("chip")
    other = lax.ppermute(operators, ("dir_1", "chip", "core"), other_half(chips))
    send, c, s = front(child_fields.reshape(64, 2, DC), patch_order, phase_angle, interp_matrix)
    received = lax.all_to_all(
        send, DIR + ("chip", "core"), 0, 0, axis_index_groups=neighbour_groups(chips), tiled=True
    )
    index = operator_index.reshape(CELLS, ENTRIES)
    chosen, done = own_operators(index, operators)
    sources, edge = to_cells(received.reshape(CELLS, WIDE + BAND), patch_order, done)
    edge, index = lax.optimization_barrier((edge, index))
    chosen_other = other_operators(index, other)
    edge = lax.ppermute(edge, "core", [(0, 1), (1, 0)])
    returned = translate(
        sources, edge, offset_code.reshape(CELLS, ENTRIES), chosen, chosen_other, patch_order
    )
    back = lax.all_to_all(returned.reshape(DBLOCKS, 8, WIDE), DIR, 0, 0, tiled=True)
    fields = anterpolate(back.reshape(8 * DBLOCKS, WIDE), interp_matrix, c, s)
    return fields.reshape(8, CHILDREN, 2, DC)


def solution(mesh):
    split = Mesh(mesh.devices.reshape(8, 2, mesh.shape["box"] // 2, 2), ("dir_0", "dir_1", "chip", "core"))
    box = ("chip", "core")
    placed = (
        P(box + DIR, None, None, None),
        P(),
        P(),
        P(box, None),
        P(box, None, None),
        P(box, None, None),
        P(None, None, DIR),
    )
    return jax.shard_map(
        per_device,
        mesh=split,
        in_specs=placed,
        out_specs=P(box + DIR, None, None, None),
        check_vma=False,
    )
```

```python
import jax
import jax.numpy as jnp
from jax import lax
from jax.experimental import pallas as pl
from jax.experimental.pallas import tpu as pltpu
from jax.sharding import Mesh
from jax.sharding import PartitionSpec as P

DC = 512
DP = 2048
CHILDREN = 8
BAND = 128
CELLS = 128
COLS = 16
ENTRIES = 40
NOPS = 128
GROUP = 16
DBLOCKS = 16
HALO = 48
WIDE = 4 * BAND
RUN = 4
TILE = 512
TILES = DP // TILE
DIR = ("dir_0", "dir_1")
F32 = jnp.float32
BF16 = jnp.bfloat16
VMEM_LIMIT = 24 * 1024 * 1024


def params():
    return pltpu.CompilerParams(vmem_limit_bytes=VMEM_LIMIT)


def cos_sin(angle):
    half = angle * 0.5
    sq = half * half
    s = F32(1.0 / 6227020800.0)
    for c in (-1.0 / 39916800.0, 1.0 / 362880.0, -1.0 / 5040.0, 1.0 / 120.0, -1.0 / 6.0, 1.0):
        s = s * sq + F32(c)
    s = s * half
    c_ = F32(1.0 / 479001600.0)
    for c in (-1.0 / 3628800.0, 1.0 / 40320.0, -1.0 / 720.0, 1.0 / 24.0, -0.5, 1.0):
        c_ = c_ * sq + F32(c)
    return 1.0 - 2.0 * s * s, 2.0 * s * c_


def block_fields(child, interp, c, s):
    prod = jnp.dot(child, interp, preferred_element_type=F32)
    re = jnp.zeros((8, prod.shape[1]), F32)
    im = re
    for k in range(CHILDREN):
        pr, pi = prod[8 * k : 8 * k + 8], prod[64 + 8 * k : 72 + 8 * k]
        ck, sk = c[k : k + 1], s[k : k + 1]
        re = re + (ck * pr - sk * pi)
        im = im + (ck * pi + sk * pr)
    columns = [slice(d * BAND, (d + 1) * BAND) for d in range(prod.shape[1] // BAND)]
    return [jnp.concatenate([re[:, at], im[:, at]], axis=1) for at in columns]


def by_part(rows):
    there = lax.broadcasted_iota(jnp.int32, (128, 128), 0)
    here = lax.broadcasted_iota(jnp.int32, (128, 128), 1)
    wanted = (there & 7) * 16 + ((there >> 3) & 7) * 2 + (there >> 6)
    pick = jnp.where(here == wanted, 1.0, 0.0).astype(BF16)
    return jnp.dot(pick, rows, preferred_element_type=F32).astype(BF16)


def by_box(rows):
    there = lax.broadcasted_iota(jnp.int32, (128, 128), 0)
    here = lax.broadcasted_iota(jnp.int32, (128, 128), 1)
    wanted = (there & 1) * 64 + ((there >> 1) & 7) * 8 + (there >> 4)
    pick = jnp.where(here == wanted, 1.0, 0.0).astype(BF16)
    return jnp.dot(pick, rows, preferred_element_type=F32).astype(BF16)


def whole():
    return pl.BlockSpec(memory_space=pltpu.VMEM)


def outer():
    return pl.BlockSpec(memory_space=pltpu.HBM)


def in_hbm(*args):
    return [pltpu.with_memory_space_constraint(x, pltpu.HBM) for x in args]


def front_kernel(
    child_hbm, order_hbm, phase_hbm, interp_hbm, send_hbm, cos_ref, sin_ref, child_ref, order_ref, phase_ref, interp_ref, send_ref, sems
):
    small = [(child_hbm, child_ref), (order_hbm, order_ref), (phase_hbm, phase_ref)]
    loads = [pltpu.make_async_copy(there, here, sems.at[k]) for k, (there, here) in enumerate(small)]
    for t in range(TILES):
        at = pl.ds(t * TILE, TILE)
        loads.append(pltpu.make_async_copy(interp_hbm.at[:, at], interp_ref.at[:, at], sems.at[len(small) + t]))
    for load in loads:
        load.start()
    loads[0].wait()
    child = by_part(child_ref[...].reshape(128, DC))
    loads[1].wait()
    order = jnp.broadcast_to(order_ref[...].astype(F32), (8, CELLS))
    loads[2].wait()
    c, s = cos_sin(phase_ref[...])
    cos_ref[...] = c
    sin_ref[...] = s
    stores = []
    for t in range(TILES):
        at = slice(t * TILE, (t + 1) * TILE)
        loads[len(small) + t].wait()
        blocks = block_fields(child, interp_ref[:, at], c[:, at], s[:, at])
        for k in range(0, len(blocks), 2):
            at = t * len(blocks) + k
            out = jnp.concatenate([blocks[k], blocks[k + 1], order], axis=1).astype(BF16)
            send_ref[at] = out
            send_ref[at + 1] = out
        here = pl.ds(t * len(blocks), len(blocks))
        stores.append(pltpu.make_async_copy(send_ref.at[here], send_hbm.at[here], sems.at[len(small) + TILES + t]))
        stores[t].start()
    for store in stores:
        store.wait()


def front(*args):
    wave = jax.ShapeDtypeStruct((CHILDREN, DP), F32)
    return pl.pallas_call(
        front_kernel,
        in_specs=[outer()] * 4,
        out_specs=[outer(), whole(), whole()],
        out_shape=(
            jax.ShapeDtypeStruct((DBLOCKS, 8, WIDE + BAND), BF16),
            wave,
            wave,
        ),
        scratch_shapes=[
            pltpu.VMEM((64, 2, DC), BF16),
            pltpu.VMEM((1, CELLS), jnp.int32),
            pltpu.VMEM((CHILDREN, DP), F32),
            pltpu.VMEM((DC, DP), BF16),
            pltpu.VMEM((DBLOCKS, 8, WIDE + BAND), BF16),
            pltpu.SemaphoreType.DMA((2 * TILES + 3,)),
        ],
        compiler_params=params(),
        cost_estimate=pl.CostEstimate(flops=2 * 128 * DC * DP, bytes_accessed=DC * DP * 2, transcendentals=0),
    )(*in_hbm(*args))


def cells_kernel(recv_ref, order_ref, sources_ref, edge_ref):
    core, half, chip = lax.axis_index("core"), lax.axis_index("dir_1"), lax.axis_index("chip")
    turned = jnp.where(core == 0, chip % RUN == 0, chip % RUN == RUN - 1).astype(jnp.int32)
    own = order_ref[...]
    ends = recv_ref[:16, WIDE:].astype(F32)
    mate = jnp.where(core == 0, ends[0:1], ends[8:9]).astype(jnp.int32)
    onehots = []
    for position, side, held in ((own, 1 - core, half), (mate, core, half ^ turned)):
        rows = (position >> 4) * 16 + side * 8 + (position & 7)
        rows = jnp.where(((position >> 3) & 1) == held, rows, -1)
        column = jnp.broadcast_to(rows.astype(F32), (BAND, BAND)).T.astype(jnp.int32)
        lanes = lax.broadcasted_iota(jnp.int32, (BAND, BAND), 1)
        onehots.append(jnp.where(column == lanes, 1.0, 0.0).astype(BF16))
    sources = jnp.dot(jnp.concatenate(onehots, axis=0), recv_ref[:, :WIDE], preferred_element_type=F32)
    sources_ref[...] = sources.astype(BF16)
    edge_ref[...] = jnp.where(core == 0, sources[CELLS - HALO : CELLS], sources[:HALO]).astype(BF16)


def to_cells(received, order):
    return pl.pallas_call(
        cells_kernel,
        in_specs=[whole()] * 2,
        out_specs=[whole()] * 2,
        out_shape=(
            jax.ShapeDtypeStruct((2 * CELLS, WIDE), BF16),
            jax.ShapeDtypeStruct((HALO, WIDE), BF16),
        ),
        compiler_params=params(),
    )(received, order)


def by_part_columns(ops):
    ops = ops.astype(F32)
    return jnp.concatenate([ops[:, 0], ops[:, 1]], axis=1).astype(BF16)


def onehot_rows(positions, width, first, rows):
    lanes = lax.broadcasted_iota(jnp.int32, (rows, width), 1)
    picks = [
        jnp.where(positions[first : first + rows, j : j + 1] == lanes, 1.0, 0.0).astype(BF16) for j in range(ENTRIES)
    ]
    return jnp.concatenate(picks, axis=0)


def added_up(fields, ops):
    re = jnp.zeros((GROUP, BAND), F32)
    im = re
    for j in range(ENTRIES):
        at = slice(j * GROUP, (j + 1) * GROUP)
        f, w = fields[at], ops[at]
        fr, fi, wr, wi = f[:, :BAND], f[:, BAND:], w[:, :BAND], w[:, BAND:]
        re = re + (wr * fr - wi * fi)
        im = im + (wr * fi + wi * fr)
    return jnp.concatenate([re, im], axis=1)


def translate_kernel(sources_ref, edge_ref, code_ref, index_ref, own_ref, other_ref, order_ref, out_ref):
    core, half = lax.axis_index("core"), lax.axis_index("dir_1")
    edge = edge_ref[...].astype(F32)
    outside = sources_ref[CELLS:].astype(F32)
    first = jnp.concatenate([edge, outside[HALO:]], axis=0)
    second = jnp.concatenate([outside[: CELLS - HALO], edge], axis=0)
    edges = jnp.where(core == 0, first, second).astype(BF16)
    sources = jnp.concatenate([sources_ref[:CELLS], edges], axis=0)
    low, high = sources[:, : 2 * BAND], sources[:, 2 * BAND :]
    own_ops, other_ops = by_part_columns(own_ref[...]), by_part_columns(other_ref[...])
    sides = (
        (low, jnp.where(half == 0, own_ops, other_ops)),
        (high, jnp.where(half == 0, other_ops, own_ops)),
    )

    code, index = code_ref[...], index_ref[...]
    cell = lax.broadcasted_iota(jnp.int32, code.shape, 0)
    up = (code * 37) >> 8
    u = (cell >> 4) + up - 3
    v = ((cell & 15) + code - 7 * up + (COLS - 3)) & 15
    source = (u & 7) * COLS + v + jnp.where((u < 0) | (u > 7), CELLS, 0)
    totals = []
    for k in range(CELLS // GROUP):
        picks = onehot_rows(source, 2 * CELLS, k * GROUP, GROUP)
        choices = onehot_rows(index, NOPS, k * GROUP, GROUP)
        both = []
        for fields, ops in sides:
            got = jnp.dot(picks, fields, preferred_element_type=F32)
            chosen = jnp.dot(choices, ops, preferred_element_type=F32)
            both.append(added_up(got, chosen))
        totals.append(jnp.concatenate(both, axis=1))
    translated = jnp.concatenate(totals, axis=0).astype(BF16)
    rows = lax.broadcasted_iota(jnp.int32, (CELLS, CELLS), 0)
    onehot = jnp.where(rows == order_ref[...], 1.0, 0.0).astype(BF16)
    out_ref[...] = jnp.dot(onehot, translated, preferred_element_type=F32).astype(BF16)


def translate(*args):
    return pl.pallas_call(
        translate_kernel,
        in_specs=[whole()] * 7,
        out_specs=whole(),
        out_shape=jax.ShapeDtypeStruct((CELLS, WIDE), BF16),
        compiler_params=params(),
    )(*args)


def anterpolate_kernel(recv_ref, interp_ref, cos_ref, sin_ref, out_ref):
    total = jnp.zeros((128, DC), F32)
    per_tile = TILE // (2 * BAND)
    for t in range(TILES):
        at = slice(t * TILE, (t + 1) * TILE)
        c, s = cos_ref[:, at], sin_ref[:, at]
        values = recv_ref[16 * per_tile * t : 16 * per_tile * (t + 1)].astype(F32)
        re, im = [], []
        for y in range(per_tile):
            both = values[16 * y : 16 * y + 8] + values[16 * y + 8 : 16 * y + 16]
            re += [both[:, :BAND], both[:, 2 * BAND : 3 * BAND]]
            im += [both[:, BAND : 2 * BAND], both[:, 3 * BAND :]]
        re, im = jnp.concatenate(re, axis=1), jnp.concatenate(im, axis=1)
        real, imag = [], []
        for k in range(CHILDREN):
            ck, sk = c[k : k + 1], s[k : k + 1]
            real.append(ck * re + sk * im)
            imag.append(ck * im - sk * re)
        shifted = jnp.concatenate(real + imag, axis=0).astype(BF16)
        total += lax.dot_general(
            shifted, interp_ref[:, at], (((1,), (1,)), ((), ())), preferred_element_type=F32
        )
    rows = by_box((total * (DC / DP)).astype(BF16))
    out_ref[...] = rows.reshape(64, 2, DC)


def anterpolate(received, interp, c, s):
    return pl.pallas_call(
        anterpolate_kernel,
        in_specs=[whole()] * 4,
        out_specs=whole(),
        out_shape=jax.ShapeDtypeStruct((64, 2, DC), BF16),
        compiler_params=params(),
    )(received, interp, c, s)


def neighbour_groups(chips):
    groups = []
    for half in range(2):
        for chip in range(chips):
            there = half ^ 1 if chip % RUN == RUN - 1 else half
            sides = ((half * chips + chip) * 2 + 1, (there * chips + (chip + 1) % chips) * 2)
            groups.append([y * 4 * chips + side for y in range(DBLOCKS // 2) for side in sides])
    return groups


def other_half(chips):
    pairs = []
    for half in range(2):
        for chip in range(chips):
            for core in range(2):
                pairs.append(((half * chips + chip) * 2 + core, ((half ^ 1) * chips + (chip ^ 2)) * 2 + core))
    return pairs


def per_device(child_fields, interp_matrix, phase_angle, patch_order, offset_code, operator_index, operators):
    chips = lax.axis_size("chip")
    other = lax.ppermute(operators, ("dir_1", "chip", "core"), other_half(chips))
    send, c, s = front(child_fields.reshape(64, 2, DC), patch_order, phase_angle, interp_matrix)
    received = lax.all_to_all(
        send, DIR + ("chip", "core"), 0, 0, axis_index_groups=neighbour_groups(chips), tiled=True
    )
    index = operator_index.reshape(CELLS, ENTRIES)
    sources, edge = to_cells(received.reshape(CELLS, WIDE + BAND), patch_order)
    edge = lax.ppermute(edge, "core", [(0, 1), (1, 0)])
    returned = translate(sources, edge, offset_code.reshape(CELLS, ENTRIES), index, operators, other, patch_order)
    back = lax.all_to_all(returned.reshape(DBLOCKS, 8, WIDE), DIR, 0, 0, tiled=True)
    fields = anterpolate(back.reshape(8 * DBLOCKS, WIDE), interp_matrix, c, s)
    return fields.reshape(8, CHILDREN, 2, DC)


def solution(mesh):
    split = Mesh(mesh.devices.reshape(8, 2, mesh.shape["box"] // 2, 2), ("dir_0", "dir_1", "chip", "core"))
    box = ("chip", "core")
    placed = (
        P(box + DIR, None, None, None),
        P(),
        P(),
        P(box, None),
        P(box, None, None),
        P(box, None, None),
        P(None, None, DIR),
    )
    return jax.shard_map(
        per_device,
        mesh=split,
        in_specs=placed,
        out_specs=P(box + DIR, None, None, None),
        check_vma=False,
    )
```

```python
import jax
import jax.numpy as jnp
from jax import lax
from jax.experimental import pallas as pl
from jax.experimental.pallas import tpu as pltpu
from jax.sharding import Mesh
from jax.sharding import PartitionSpec as P

DC = 512
DP = 2048
CHILDREN = 8
BAND = 128
CELLS = 128
COLS = 16
ENTRIES = 40
NOPS = 128
GROUP = 16
DBLOCKS = 16
HALO = 48
WIDE = 4 * BAND
RUN = 4
TILE = 512
TILES = DP // TILE
FRONT_TILE = 1024
FRONT_TILES = DP // FRONT_TILE
DIR = ("dir_0", "dir_1")
F32 = jnp.float32
BF16 = jnp.bfloat16
VMEM_LIMIT = 24 * 1024 * 1024


def params():
    return pltpu.CompilerParams(vmem_limit_bytes=VMEM_LIMIT)


def cos_sin(angle):
    half = angle * 0.5
    sq = half * half
    s = F32(1.0 / 6227020800.0)
    for c in (-1.0 / 39916800.0, 1.0 / 362880.0, -1.0 / 5040.0, 1.0 / 120.0, -1.0 / 6.0, 1.0):
        s = s * sq + F32(c)
    s = s * half
    c_ = F32(1.0 / 479001600.0)
    for c in (-1.0 / 3628800.0, 1.0 / 40320.0, -1.0 / 720.0, 1.0 / 24.0, -0.5, 1.0):
        c_ = c_ * sq + F32(c)
    return 1.0 - 2.0 * s * s, 2.0 * s * c_


def block_fields(child, interp, c, s):
    prod = jnp.dot(child, interp, preferred_element_type=F32)
    re = jnp.zeros((8, prod.shape[1]), F32)
    im = re
    for k in range(CHILDREN):
        pr, pi = prod[8 * k : 8 * k + 8], prod[64 + 8 * k : 72 + 8 * k]
        ck, sk = c[k : k + 1], s[k : k + 1]
        re = re + (ck * pr - sk * pi)
        im = im + (ck * pi + sk * pr)
    columns = [slice(d * BAND, (d + 1) * BAND) for d in range(prod.shape[1] // BAND)]
    return [jnp.concatenate([re[:, at], im[:, at]], axis=1) for at in columns]


def by_part(rows):
    there = lax.broadcasted_iota(jnp.int32, (128, 128), 0)
    here = lax.broadcasted_iota(jnp.int32, (128, 128), 1)
    wanted = (there & 7) * 16 + ((there >> 3) & 7) * 2 + (there >> 6)
    pick = jnp.where(here == wanted, 1.0, 0.0).astype(BF16)
    return jnp.dot(pick, rows, preferred_element_type=F32).astype(BF16)


def by_box(rows):
    there = lax.broadcasted_iota(jnp.int32, (128, 128), 0)
    here = lax.broadcasted_iota(jnp.int32, (128, 128), 1)
    wanted = (there & 1) * 64 + ((there >> 1) & 7) * 8 + (there >> 4)
    pick = jnp.where(here == wanted, 1.0, 0.0).astype(BF16)
    return jnp.dot(pick, rows, preferred_element_type=F32).astype(BF16)


def whole():
    return pl.BlockSpec(memory_space=pltpu.VMEM)


def outer():
    return pl.BlockSpec(memory_space=pltpu.HBM)


def in_hbm(*args):
    return [pltpu.with_memory_space_constraint(x, pltpu.HBM) for x in args]


def front_kernel(
    child_hbm, order_hbm, phase_hbm, interp_hbm, send_hbm, cos_ref, sin_ref, child_ref, order_ref, phase_ref, interp_ref, send_ref, sems
):
    small = [(child_hbm, child_ref), (order_hbm, order_ref), (phase_hbm, phase_ref)]
    loads = [pltpu.make_async_copy(there, here, sems.at[k]) for k, (there, here) in enumerate(small)]
    for t in range(FRONT_TILES):
        at = pl.ds(t * FRONT_TILE, FRONT_TILE)
        loads.append(pltpu.make_async_copy(interp_hbm.at[:, at], interp_ref.at[:, at], sems.at[len(small) + t]))
    for load in loads:
        load.start()
    loads[0].wait()
    child = by_part(child_ref[...].reshape(128, DC))
    loads[1].wait()
    order = jnp.broadcast_to(order_ref[...].astype(F32), (8, CELLS))
    loads[2].wait()
    c, s = cos_sin(phase_ref[...])
    cos_ref[...] = c
    sin_ref[...] = s
    stores = []
    for t in range(FRONT_TILES):
        at = slice(t * FRONT_TILE, (t + 1) * FRONT_TILE)
        loads[len(small) + t].wait()
        blocks = block_fields(child, interp_ref[:, at], c[:, at], s[:, at])
        for k in range(0, len(blocks), 2):
            at = t * len(blocks) + k
            out = jnp.concatenate([blocks[k], blocks[k + 1], order], axis=1).astype(BF16)
            send_ref[at] = out
            send_ref[at + 1] = out
        here = pl.ds(t * len(blocks), len(blocks))
        stores.append(pltpu.make_async_copy(send_ref.at[here], send_hbm.at[here], sems.at[len(small) + FRONT_TILES + t]))
        stores[t].start()
    for store in stores:
        store.wait()


def front(*args):
    wave = jax.ShapeDtypeStruct((CHILDREN, DP), F32)
    return pl.pallas_call(
        front_kernel,
        in_specs=[outer()] * 4,
        out_specs=[outer(), whole(), whole()],
        out_shape=(
            jax.ShapeDtypeStruct((DBLOCKS, 8, WIDE + BAND), BF16),
            wave,
            wave,
        ),
        scratch_shapes=[
            pltpu.VMEM((64, 2, DC), BF16),
            pltpu.VMEM((1, CELLS), jnp.int32),
            pltpu.VMEM((CHILDREN, DP), F32),
            pltpu.VMEM((DC, DP), BF16),
            pltpu.VMEM((DBLOCKS, 8, WIDE + BAND), BF16),
            pltpu.SemaphoreType.DMA((2 * FRONT_TILES + 3,)),
        ],
        compiler_params=params(),
        cost_estimate=pl.CostEstimate(flops=2 * 128 * DC * DP, bytes_accessed=DC * DP * 2, transcendentals=0),
    )(*in_hbm(*args))


def cells_kernel(recv_ref, order_ref, sources_ref, edge_ref):
    core, half, chip = lax.axis_index("core"), lax.axis_index("dir_1"), lax.axis_index("chip")
    turned = jnp.where(core == 0, chip % RUN == 0, chip % RUN == RUN - 1).astype(jnp.int32)
    own = order_ref[...]
    ends = recv_ref[:16, WIDE:].astype(F32)
    mate = jnp.where(core == 0, ends[0:1], ends[8:9]).astype(jnp.int32)
    onehots = []
    for position, side, held in ((own, 1 - core, half), (mate, core, half ^ turned)):
        rows = (position >> 4) * 16 + side * 8 + (position & 7)
        rows = jnp.where(((position >> 3) & 1) == held, rows, -1)
        column = jnp.broadcast_to(rows.astype(F32), (BAND, BAND)).T.astype(jnp.int32)
        lanes = lax.broadcasted_iota(jnp.int32, (BAND, BAND), 1)
        onehots.append(jnp.where(column == lanes, 1.0, 0.0).astype(BF16))
    sources = jnp.dot(jnp.concatenate(onehots, axis=0), recv_ref[:, :WIDE], preferred_element_type=F32)
    sources_ref[...] = sources.astype(BF16)
    edge_ref[...] = jnp.where(core == 0, sources[CELLS - HALO : CELLS], sources[:HALO]).astype(BF16)


def to_cells(received, order):
    return pl.pallas_call(
        cells_kernel,
        in_specs=[whole()] * 2,
        out_specs=[whole()] * 2,
        out_shape=(
            jax.ShapeDtypeStruct((2 * CELLS, WIDE), BF16),
            jax.ShapeDtypeStruct((HALO, WIDE), BF16),
        ),
        compiler_params=params(),
    )(received, order)


def by_part_columns(ops):
    ops = ops.astype(F32)
    return jnp.concatenate([ops[:, 0], ops[:, 1]], axis=1).astype(BF16)


def onehot_rows(positions, width, first, rows):
    lanes = lax.broadcasted_iota(jnp.int32, (rows, width), 1)
    picks = [
        jnp.where(positions[first : first + rows, j : j + 1] == lanes, 1.0, 0.0).astype(BF16) for j in range(ENTRIES)
    ]
    return jnp.concatenate(picks, axis=0)


def added_up(fields, ops):
    re = jnp.zeros((GROUP, BAND), F32)
    im = re
    for j in range(ENTRIES):
        at = slice(j * GROUP, (j + 1) * GROUP)
        f, w = fields[at], ops[at]
        fr, fi, wr, wi = f[:, :BAND], f[:, BAND:], w[:, :BAND], w[:, BAND:]
        re = re + (wr * fr - wi * fi)
        im = im + (wr * fi + wi * fr)
    return jnp.concatenate([re, im], axis=1)


def translate_kernel(sources_ref, edge_ref, code_ref, index_ref, own_ref, other_ref, order_ref, out_ref):
    core, half = lax.axis_index("core"), lax.axis_index("dir_1")
    edge = edge_ref[...].astype(F32)
    outside = sources_ref[CELLS:].astype(F32)
    first = jnp.concatenate([edge, outside[HALO:]], axis=0)
    second = jnp.concatenate([outside[: CELLS - HALO], edge], axis=0)
    edges = jnp.where(core == 0, first, second).astype(BF16)
    sources = jnp.concatenate([sources_ref[:CELLS], edges], axis=0)
    low, high = sources[:, : 2 * BAND], sources[:, 2 * BAND :]
    own_ops, other_ops = by_part_columns(own_ref[...]), by_part_columns(other_ref[...])
    sides = (
        (low, jnp.where(half == 0, own_ops, other_ops)),
        (high, jnp.where(half == 0, other_ops, own_ops)),
    )

    code, index = code_ref[...], index_ref[...]
    cell = lax.broadcasted_iota(jnp.int32, code.shape, 0)
    up = (code * 37) >> 8
    u = (cell >> 4) + up - 3
    v = ((cell & 15) + code - 7 * up + (COLS - 3)) & 15
    source = (u & 7) * COLS + v + jnp.where((u < 0) | (u > 7), CELLS, 0)
    totals = []
    for k in range(CELLS // GROUP):
        picks = onehot_rows(source, 2 * CELLS, k * GROUP, GROUP)
        choices = onehot_rows(index, NOPS, k * GROUP, GROUP)
        both = []
        for fields, ops in sides:
            got = jnp.dot(picks, fields, preferred_element_type=F32)
            chosen = jnp.dot(choices, ops, preferred_element_type=F32)
            both.append(added_up(got, chosen))
        totals.append(jnp.concatenate(both, axis=1))
    translated = jnp.concatenate(totals, axis=0).astype(BF16)
    rows = lax.broadcasted_iota(jnp.int32, (CELLS, CELLS), 0)
    place = order_ref[...]
    place = ((place >> 3) & 1) * 64 + (place >> 4) * 8 + (place & 7)
    onehot = jnp.where(rows == place, 1.0, 0.0).astype(BF16)
    out_ref[...] = jnp.dot(onehot, translated, preferred_element_type=F32).astype(BF16)


def translate(*args):
    return pl.pallas_call(
        translate_kernel,
        in_specs=[whole()] * 7,
        out_specs=whole(),
        out_shape=jax.ShapeDtypeStruct((CELLS, WIDE), BF16),
        compiler_params=params(),
    )(*args)


def anterpolate_kernel(recv_ref, interp_ref, cos_ref, sin_ref, out_ref):
    total = jnp.zeros((128, DC), F32)
    per_tile = TILE // (2 * BAND)
    halves = recv_ref[...].astype(F32).reshape(2, 64, WIDE)
    for t in range(TILES):
        at = slice(t * TILE, (t + 1) * TILE)
        c, s = cos_ref[:, at], sin_ref[:, at]
        rows = slice(8 * per_tile * t, 8 * per_tile * (t + 1))
        values = halves[0, rows] + halves[1, rows]
        re, im = [], []
        for y in range(per_tile):
            both = values[8 * y : 8 * y + 8]
            re += [both[:, :BAND], both[:, 2 * BAND : 3 * BAND]]
            im += [both[:, BAND : 2 * BAND], both[:, 3 * BAND :]]
        re, im = jnp.concatenate(re, axis=1), jnp.concatenate(im, axis=1)
        real, imag = [], []
        for k in range(CHILDREN):
            ck, sk = c[k : k + 1], s[k : k + 1]
            real.append(ck * re + sk * im)
            imag.append(ck * im - sk * re)
        shifted = jnp.concatenate(real + imag, axis=0).astype(BF16)
        total += lax.dot_general(
            shifted, interp_ref[:, at], (((1,), (1,)), ((), ())), preferred_element_type=F32
        )
    rows = by_box((total * (DC / DP)).astype(BF16))
    out_ref[...] = rows.reshape(64, 2, DC)


def anterpolate(received, interp, c, s):
    return pl.pallas_call(
        anterpolate_kernel,
        in_specs=[whole()] * 4,
        out_specs=whole(),
        out_shape=jax.ShapeDtypeStruct((64, 2, DC), BF16),
        compiler_params=params(),
    )(received, interp, c, s)


def neighbour_groups(chips):
    groups = []
    for half in range(2):
        for chip in range(chips):
            there = half ^ 1 if chip % RUN == RUN - 1 else half
            sides = ((half * chips + chip) * 2 + 1, (there * chips + (chip + 1) % chips) * 2)
            groups.append([y * 4 * chips + side for y in range(DBLOCKS // 2) for side in sides])
    return groups


def patch_groups(chips):
    size = 2 * chips
    return [[(2 * y + half) * size + box for half in range(2) for y in range(DBLOCKS // 2)] for box in range(size)]


def other_half(chips):
    pairs = []
    for half in range(2):
        for chip in range(chips):
            for core in range(2):
                pairs.append(((half * chips + chip) * 2 + core, ((half ^ 1) * chips + (chip ^ 2)) * 2 + core))
    return pairs


def per_device(child_fields, interp_matrix, phase_angle, patch_order, offset_code, operator_index, operators):
    chips = lax.axis_size("chip")
    other = lax.ppermute(operators, ("dir_1", "chip", "core"), other_half(chips))
    send, c, s = front(child_fields.reshape(64, 2, DC), patch_order, phase_angle, interp_matrix)
    received = lax.all_to_all(
        send, DIR + ("chip", "core"), 0, 0, axis_index_groups=neighbour_groups(chips), tiled=True
    )
    index = operator_index.reshape(CELLS, ENTRIES)
    sources, edge = to_cells(received.reshape(CELLS, WIDE + BAND), patch_order)
    edge = lax.ppermute(edge, "core", [(0, 1), (1, 0)])
    returned = translate(sources, edge, offset_code.reshape(CELLS, ENTRIES), index, operators, other, patch_order)
    back = lax.all_to_all(
        returned.reshape(DBLOCKS, 8, WIDE), DIR + ("chip", "core"), 0, 0, axis_index_groups=patch_groups(chips), tiled=True
    )
    fields = anterpolate(back.reshape(8 * DBLOCKS, WIDE), interp_matrix, c, s)
    return fields.reshape(8, CHILDREN, 2, DC)


def solution(mesh):
    split = Mesh(mesh.devices.reshape(8, 2, mesh.shape["box"] // 2, 2), ("dir_0", "dir_1", "chip", "core"))
    box = ("chip", "core")
    placed = (
        P(box + DIR, None, None, None),
        P(),
        P(),
        P(box, None),
        P(box, None, None),
        P(box, None, None),
        P(None, None, DIR),
    )
    return jax.shard_map(
        per_device,
        mesh=split,
        in_specs=placed,
        out_specs=P(box + DIR, None, None, None),
        check_vma=False,
    )
```

```python
import jax
import jax.numpy as jnp
from jax import lax
from jax.experimental import pallas as pl
from jax.experimental.pallas import tpu as pltpu
from jax.sharding import Mesh
from jax.sharding import PartitionSpec as P

DC = 512
DP = 2048
CHILDREN = 8
BAND = 128
CELLS = 128
COLS = 16
ENTRIES = 40
NOPS = 128
GROUP = 16
DBLOCKS = 16
HALO = 48
WIDE = 4 * BAND
RUN = 4
TILE = 512
TILES = DP // TILE
FRONT_TILE = 1024
FRONT_TILES = DP // FRONT_TILE
DIR = ("dir_0", "dir_1")
F32 = jnp.float32
BF16 = jnp.bfloat16
VMEM_LIMIT = 24 * 1024 * 1024


def params():
    return pltpu.CompilerParams(vmem_limit_bytes=VMEM_LIMIT)


def cos_sin(angle):
    half = angle * 0.5
    sq = half * half
    s = F32(1.0 / 6227020800.0)
    for c in (-1.0 / 39916800.0, 1.0 / 362880.0, -1.0 / 5040.0, 1.0 / 120.0, -1.0 / 6.0, 1.0):
        s = s * sq + F32(c)
    s = s * half
    c_ = F32(1.0 / 479001600.0)
    for c in (-1.0 / 3628800.0, 1.0 / 40320.0, -1.0 / 720.0, 1.0 / 24.0, -0.5, 1.0):
        c_ = c_ * sq + F32(c)
    return 1.0 - 2.0 * s * s, 2.0 * s * c_


def block_fields(child, interp, c, s):
    prod = jnp.dot(child, interp, preferred_element_type=F32)
    re = jnp.zeros((8, prod.shape[1]), F32)
    im = re
    for k in range(CHILDREN):
        pr, pi = prod[8 * k : 8 * k + 8], prod[64 + 8 * k : 72 + 8 * k]
        ck, sk = c[k : k + 1], s[k : k + 1]
        re = re + (ck * pr - sk * pi)
        im = im + (ck * pi + sk * pr)
    columns = [slice(d * BAND, (d + 1) * BAND) for d in range(prod.shape[1] // BAND)]
    return [jnp.concatenate([re[:, at], im[:, at]], axis=1) for at in columns]


def by_part(rows):
    there = lax.broadcasted_iota(jnp.int32, (128, 128), 0)
    here = lax.broadcasted_iota(jnp.int32, (128, 128), 1)
    wanted = (there & 7) * 16 + ((there >> 3) & 7) * 2 + (there >> 6)
    pick = jnp.where(here == wanted, 1.0, 0.0).astype(BF16)
    return jnp.dot(pick, rows, preferred_element_type=F32).astype(BF16)


def by_box(rows):
    there = lax.broadcasted_iota(jnp.int32, (128, 128), 0)
    here = lax.broadcasted_iota(jnp.int32, (128, 128), 1)
    wanted = (there & 1) * 64 + ((there >> 1) & 7) * 8 + (there >> 4)
    pick = jnp.where(here == wanted, 1.0, 0.0).astype(BF16)
    return jnp.dot(pick, rows, preferred_element_type=F32).astype(BF16)


def whole():
    return pl.BlockSpec(memory_space=pltpu.VMEM)


def outer():
    return pl.BlockSpec(memory_space=pltpu.HBM)


def in_hbm(*args):
    return [pltpu.with_memory_space_constraint(x, pltpu.HBM) for x in args]


def front_kernel(
    child_hbm, order_hbm, phase_hbm, interp_hbm, send_hbm, cos_ref, sin_ref, child_ref, order_ref, phase_ref, interp_ref, send_ref, sems
):
    small = [(child_hbm, child_ref), (order_hbm, order_ref), (phase_hbm, phase_ref)]
    loads = [pltpu.make_async_copy(there, here, sems.at[k]) for k, (there, here) in enumerate(small)]
    for t in range(FRONT_TILES):
        at = pl.ds(t * FRONT_TILE, FRONT_TILE)
        loads.append(pltpu.make_async_copy(interp_hbm.at[:, at], interp_ref.at[:, at], sems.at[len(small) + t]))
    for load in loads:
        load.start()
    loads[0].wait()
    child = by_part(child_ref[...].reshape(128, DC))
    loads[1].wait()
    order = jnp.broadcast_to(order_ref[...].astype(F32), (8, CELLS))
    loads[2].wait()
    c, s = cos_sin(phase_ref[...])
    cos_ref[...] = c
    sin_ref[...] = s
    stores = []
    for t in range(FRONT_TILES):
        at = slice(t * FRONT_TILE, (t + 1) * FRONT_TILE)
        loads[len(small) + t].wait()
        blocks = block_fields(child, interp_ref[:, at], c[:, at], s[:, at])
        for k in range(0, len(blocks), 2):
            at = t * len(blocks) + k
            out = jnp.concatenate([blocks[k], blocks[k + 1], order], axis=1).astype(BF16)
            send_ref[at] = out
            send_ref[at + 1] = out
        here = pl.ds(t * len(blocks), len(blocks))
        stores.append(pltpu.make_async_copy(send_ref.at[here], send_hbm.at[here], sems.at[len(small) + FRONT_TILES + t]))
        stores[t].start()
    for store in stores:
        store.wait()


def front(*args):
    wave = jax.ShapeDtypeStruct((CHILDREN, DP), F32)
    return pl.pallas_call(
        front_kernel,
        in_specs=[outer()] * 4,
        out_specs=[outer(), whole(), whole()],
        out_shape=(
            jax.ShapeDtypeStruct((DBLOCKS, 8, WIDE + BAND), BF16),
            wave,
            wave,
        ),
        scratch_shapes=[
            pltpu.VMEM((64, 2, DC), BF16),
            pltpu.VMEM((1, CELLS), jnp.int32),
            pltpu.VMEM((CHILDREN, DP), F32),
            pltpu.VMEM((DC, DP), BF16),
            pltpu.VMEM((DBLOCKS, 8, WIDE + BAND), BF16),
            pltpu.SemaphoreType.DMA((2 * FRONT_TILES + 3,)),
        ],
        compiler_params=params(),
        cost_estimate=pl.CostEstimate(flops=2 * 128 * DC * DP, bytes_accessed=DC * DP * 2, transcendentals=0),
    )(*in_hbm(*args))


def cells_kernel(recv_ref, order_ref, sources_ref, edge_ref):
    core, half, chip = lax.axis_index("core"), lax.axis_index("dir_1"), lax.axis_index("chip")
    turned = jnp.where(core == 0, chip % RUN == 0, chip % RUN == RUN - 1).astype(jnp.int32)
    own = order_ref[...]
    ends = recv_ref[:16, WIDE:].astype(F32)
    mate = jnp.where(core == 0, ends[0:1], ends[8:9]).astype(jnp.int32)
    onehots = []
    for position, side, held in ((own, 1 - core, half), (mate, core, half ^ turned)):
        rows = (position >> 4) * 16 + side * 8 + (position & 7)
        rows = jnp.where(((position >> 3) & 1) == held, rows, -1)
        column = jnp.broadcast_to(rows.astype(F32), (BAND, BAND)).T.astype(jnp.int32)
        lanes = lax.broadcasted_iota(jnp.int32, (BAND, BAND), 1)
        onehots.append(jnp.where(column == lanes, 1.0, 0.0).astype(BF16))
    sources = jnp.dot(jnp.concatenate(onehots, axis=0), recv_ref[:, :WIDE], preferred_element_type=F32)
    sources_ref[...] = sources.astype(BF16)
    edge_ref[...] = jnp.where(core == 0, sources[CELLS - HALO : CELLS], sources[:HALO]).astype(BF16)


def to_cells(received, order):
    return pl.pallas_call(
        cells_kernel,
        in_specs=[whole()] * 2,
        out_specs=[whole()] * 2,
        out_shape=(
            jax.ShapeDtypeStruct((2 * CELLS, WIDE), BF16),
            jax.ShapeDtypeStruct((HALO, WIDE), BF16),
        ),
        compiler_params=params(),
    )(received, order)


def by_part_columns(ops):
    ops = ops.astype(F32)
    return jnp.concatenate([ops[:, 0], ops[:, 1]], axis=1).astype(BF16)


def onehot_rows(positions, width, first, rows):
    lanes = lax.broadcasted_iota(jnp.int32, (rows, width), 1)
    picks = [
        jnp.where(positions[first : first + rows, j : j + 1] == lanes, 1.0, 0.0).astype(BF16) for j in range(ENTRIES)
    ]
    return jnp.concatenate(picks, axis=0)


def added_up(fields, ops):
    re = jnp.zeros((GROUP, BAND), F32)
    im = re
    for j in range(ENTRIES):
        at = slice(j * GROUP, (j + 1) * GROUP)
        f, w = fields[at], ops[at]
        fr, fi, wr, wi = f[:, :BAND], f[:, BAND:], w[:, :BAND], w[:, BAND:]
        re = re + (wr * fr - wi * fi)
        im = im + (wr * fi + wi * fr)
    return jnp.concatenate([re, im], axis=1)


def translate_kernel(sources_ref, edge_ref, code_ref, index_ref, own_ref, other_ref, order_ref, out_ref):
    core, half = lax.axis_index("core"), lax.axis_index("dir_1")
    edge = edge_ref[...].astype(F32)
    outside = sources_ref[CELLS:].astype(F32)
    first = jnp.concatenate([edge, outside[HALO:]], axis=0)
    second = jnp.concatenate([outside[: CELLS - HALO], edge], axis=0)
    edges = jnp.where(core == 0, first, second).astype(BF16)
    sources = jnp.concatenate([sources_ref[:CELLS], edges], axis=0)
    low, high = sources[:, : 2 * BAND], sources[:, 2 * BAND :]
    own_ops, other_ops = by_part_columns(own_ref[...]), by_part_columns(other_ref[...])
    sides = (
        (low, jnp.where(half == 0, own_ops, other_ops)),
        (high, jnp.where(half == 0, other_ops, own_ops)),
    )

    code, index = code_ref[...], index_ref[...]
    cell = lax.broadcasted_iota(jnp.int32, code.shape, 0)
    up = (code * 37) >> 8
    u = (cell >> 4) + up - 3
    v = ((cell & 15) + code - 7 * up + (COLS - 3)) & 15
    source = (u & 7) * COLS + v + jnp.where((u < 0) | (u > 7), CELLS, 0)
    totals = []
    for k in range(CELLS // GROUP):
        picks = onehot_rows(source, 2 * CELLS, k * GROUP, GROUP)
        choices = onehot_rows(index, NOPS, k * GROUP, GROUP)
        both = []
        for fields, ops in sides:
            got = jnp.dot(picks, fields, preferred_element_type=F32)
            chosen = jnp.dot(choices, ops, preferred_element_type=F32)
            both.append(added_up(got, chosen))
        totals.append(jnp.concatenate(both, axis=1))
    translated = jnp.concatenate(totals, axis=0).astype(BF16)
    rows = lax.broadcasted_iota(jnp.int32, (CELLS, CELLS), 0)
    place = order_ref[...]
    place = ((place >> 3) & 1) * 64 + (place >> 4) * 8 + (place & 7)
    onehot = jnp.where(rows == place, 1.0, 0.0).astype(BF16)
    out_ref[...] = jnp.dot(onehot, translated, preferred_element_type=F32).astype(BF16)


def translate(*args):
    return pl.pallas_call(
        translate_kernel,
        in_specs=[whole()] * 7,
        out_specs=whole(),
        out_shape=jax.ShapeDtypeStruct((CELLS, WIDE), BF16),
        compiler_params=params(),
    )(*args)


def anterpolate_kernel(recv_ref, interp_ref, cos_ref, sin_ref, out_hbm, out_ref, sems):
    shifted = []
    per_tile = TILE // (2 * BAND)
    halves = recv_ref[...].astype(F32).reshape(2, 64, WIDE)
    for t in range(TILES):
        at = slice(t * TILE, (t + 1) * TILE)
        c, s = cos_ref[:, at], sin_ref[:, at]
        rows = slice(8 * per_tile * t, 8 * per_tile * (t + 1))
        values = halves[0, rows] + halves[1, rows]
        re, im = [], []
        for y in range(per_tile):
            both = values[8 * y : 8 * y + 8]
            re += [both[:, :BAND], both[:, 2 * BAND : 3 * BAND]]
            im += [both[:, BAND : 2 * BAND], both[:, 3 * BAND :]]
        re, im = jnp.concatenate(re, axis=1), jnp.concatenate(im, axis=1)
        real, imag = [], []
        for k in range(CHILDREN):
            ck, sk = c[k : k + 1], s[k : k + 1]
            real.append(ck * re + sk * im)
            imag.append(ck * im - sk * re)
        shifted.append(jnp.concatenate(real + imag, axis=0).astype(BF16))
    shifted = jnp.concatenate(shifted, axis=1)
    stores = []
    for n in range(2):
        at = slice(n * DC // 2, (n + 1) * DC // 2)
        total = lax.dot_general(shifted, interp_ref[at], (((1,), (1,)), ((), ())), preferred_element_type=F32)
        out_ref[n] = by_box((total * (DC / DP)).astype(BF16)).reshape(64, 2, DC // 2)
        there = out_hbm.at[:, :, pl.ds(n * DC // 2, DC // 2)]
        stores.append(pltpu.make_async_copy(out_ref.at[n], there, sems.at[n]))
        stores[n].start()
    for store in stores:
        store.wait()


def anterpolate(received, interp, c, s):
    return pl.pallas_call(
        anterpolate_kernel,
        in_specs=[whole()] * 4,
        out_specs=outer(),
        out_shape=jax.ShapeDtypeStruct((64, 2, DC), BF16),
        scratch_shapes=[pltpu.VMEM((2, 64, 2, DC // 2), BF16), pltpu.SemaphoreType.DMA((2,))],
        compiler_params=params(),
    )(received, interp, c, s)


def neighbour_groups(chips):
    groups = []
    for half in range(2):
        for chip in range(chips):
            there = half ^ 1 if chip % RUN == RUN - 1 else half
            sides = ((half * chips + chip) * 2 + 1, (there * chips + (chip + 1) % chips) * 2)
            groups.append([y * 4 * chips + side for y in range(DBLOCKS // 2) for side in sides])
    return groups


def patch_groups(chips):
    size = 2 * chips
    return [[(2 * y + half) * size + box for half in range(2) for y in range(DBLOCKS // 2)] for box in range(size)]


def other_half(chips):
    pairs = []
    for half in range(2):
        for chip in range(chips):
            for core in range(2):
                pairs.append(((half * chips + chip) * 2 + core, ((half ^ 1) * chips + (chip ^ 2)) * 2 + core))
    return pairs


def per_device(child_fields, interp_matrix, phase_angle, patch_order, offset_code, operator_index, operators):
    chips = lax.axis_size("chip")
    other = lax.ppermute(operators, ("dir_1", "chip", "core"), other_half(chips))
    send, c, s = front(child_fields.reshape(64, 2, DC), patch_order, phase_angle, interp_matrix)
    received = lax.all_to_all(
        send, DIR + ("chip", "core"), 0, 0, axis_index_groups=neighbour_groups(chips), tiled=True
    )
    index = operator_index.reshape(CELLS, ENTRIES)
    sources, edge = to_cells(received.reshape(CELLS, WIDE + BAND), patch_order)
    edge = lax.ppermute(edge, "core", [(0, 1), (1, 0)])
    returned = translate(sources, edge, offset_code.reshape(CELLS, ENTRIES), index, operators, other, patch_order)
    back = lax.all_to_all(
        returned.reshape(DBLOCKS, 8, WIDE), DIR + ("chip", "core"), 0, 0, axis_index_groups=patch_groups(chips), tiled=True
    )
    fields = anterpolate(back.reshape(8 * DBLOCKS, WIDE), interp_matrix, c, s)
    return fields.reshape(8, CHILDREN, 2, DC)


def solution(mesh):
    split = Mesh(mesh.devices.reshape(8, 2, mesh.shape["box"] // 2, 2), ("dir_0", "dir_1", "chip", "core"))
    box = ("chip", "core")
    placed = (
        P(box + DIR, None, None, None),
        P(),
        P(),
        P(box, None),
        P(box, None, None),
        P(box, None, None),
        P(None, None, DIR),
    )
    return jax.shard_map(
        per_device,
        mesh=split,
        in_specs=placed,
        out_specs=P(box + DIR, None, None, None),
        check_vma=False,
    )
```

```python
import jax
import jax.numpy as jnp
from jax import lax
from jax.experimental import pallas as pl
from jax.experimental.pallas import tpu as pltpu
from jax.sharding import Mesh
from jax.sharding import PartitionSpec as P

DC = 512
DP = 2048
CHILDREN = 8
BAND = 128
CELLS = 128
COLS = 16
ENTRIES = 40
NOPS = 128
GROUP = 16
DBLOCKS = 16
HALO = 48
WIDE = 4 * BAND
RUN = 4
TILE = 1024
TILES = DP // TILE
FRONT_TILE = 1024
FRONT_TILES = DP // FRONT_TILE
DIR = ("dir_0", "dir_1")
F32 = jnp.float32
BF16 = jnp.bfloat16
VMEM_LIMIT = 24 * 1024 * 1024


def params():
    return pltpu.CompilerParams(vmem_limit_bytes=VMEM_LIMIT)


def cos_sin(angle):
    half = angle * 0.5
    sq = half * half
    s = F32(1.0 / 6227020800.0)
    for c in (-1.0 / 39916800.0, 1.0 / 362880.0, -1.0 / 5040.0, 1.0 / 120.0, -1.0 / 6.0, 1.0):
        s = s * sq + F32(c)
    s = s * half
    c_ = F32(1.0 / 479001600.0)
    for c in (-1.0 / 3628800.0, 1.0 / 40320.0, -1.0 / 720.0, 1.0 / 24.0, -0.5, 1.0):
        c_ = c_ * sq + F32(c)
    return 1.0 - 2.0 * s * s, 2.0 * s * c_


def block_fields(child, interp, c, s):
    prod = jnp.dot(child, interp, preferred_element_type=F32)
    re = jnp.zeros((8, prod.shape[1]), F32)
    im = re
    for k in range(CHILDREN):
        pr, pi = prod[8 * k : 8 * k + 8], prod[64 + 8 * k : 72 + 8 * k]
        ck, sk = c[k : k + 1], s[k : k + 1]
        re = re + (ck * pr - sk * pi)
        im = im + (ck * pi + sk * pr)
    columns = [slice(d * BAND, (d + 1) * BAND) for d in range(prod.shape[1] // BAND)]
    return [jnp.concatenate([re[:, at], im[:, at]], axis=1) for at in columns]


def by_part(rows):
    there = lax.broadcasted_iota(jnp.int32, (128, 128), 0)
    here = lax.broadcasted_iota(jnp.int32, (128, 128), 1)
    wanted = (there & 7) * 16 + ((there >> 3) & 7) * 2 + (there >> 6)
    pick = jnp.where(here == wanted, 1.0, 0.0).astype(BF16)
    return jnp.dot(pick, rows, preferred_element_type=F32).astype(BF16)


def by_box(rows):
    there = lax.broadcasted_iota(jnp.int32, (128, 128), 0)
    here = lax.broadcasted_iota(jnp.int32, (128, 128), 1)
    wanted = (there & 1) * 64 + ((there >> 1) & 7) * 8 + (there >> 4)
    pick = jnp.where(here == wanted, 1.0, 0.0).astype(BF16)
    return jnp.dot(pick, rows, preferred_element_type=F32).astype(BF16)


def whole():
    return pl.BlockSpec(memory_space=pltpu.VMEM)


def outer():
    return pl.BlockSpec(memory_space=pltpu.HBM)


def in_hbm(*args):
    return [pltpu.with_memory_space_constraint(x, pltpu.HBM) for x in args]


def front_kernel(
    child_hbm, order_hbm, phase_hbm, interp_hbm, send_hbm, cos_ref, sin_ref, child_ref, order_ref, phase_ref, interp_ref, send_ref, sems
):
    small = [(child_hbm, child_ref), (order_hbm, order_ref), (phase_hbm, phase_ref)]
    loads = [pltpu.make_async_copy(there, here, sems.at[k]) for k, (there, here) in enumerate(small)]
    for t in range(FRONT_TILES):
        at = pl.ds(t * FRONT_TILE, FRONT_TILE)
        loads.append(pltpu.make_async_copy(interp_hbm.at[:, at], interp_ref.at[:, at], sems.at[len(small) + t]))
    for load in loads:
        load.start()
    loads[0].wait()
    child = by_part(child_ref[...].reshape(128, DC))
    loads[1].wait()
    order = jnp.broadcast_to(order_ref[...].astype(F32), (8, CELLS))
    loads[2].wait()
    c, s = cos_sin(phase_ref[...])
    cos_ref[...] = c
    sin_ref[...] = s
    stores = []
    for t in range(FRONT_TILES):
        at = slice(t * FRONT_TILE, (t + 1) * FRONT_TILE)
        loads[len(small) + t].wait()
        blocks = block_fields(child, interp_ref[:, at], c[:, at], s[:, at])
        for k in range(0, len(blocks), 2):
            at = t * len(blocks) + k
            out = jnp.concatenate([blocks[k], blocks[k + 1], order], axis=1).astype(BF16)
            send_ref[at] = out
            send_ref[at + 1] = out
        here = pl.ds(t * len(blocks), len(blocks))
        stores.append(pltpu.make_async_copy(send_ref.at[here], send_hbm.at[here], sems.at[len(small) + FRONT_TILES + t]))
        stores[t].start()
    for store in stores:
        store.wait()


def front(*args):
    wave = jax.ShapeDtypeStruct((CHILDREN, DP), F32)
    return pl.pallas_call(
        front_kernel,
        in_specs=[outer()] * 4,
        out_specs=[outer(), whole(), whole()],
        out_shape=(
            jax.ShapeDtypeStruct((DBLOCKS, 8, WIDE + BAND), BF16),
            wave,
            wave,
        ),
        scratch_shapes=[
            pltpu.VMEM((64, 2, DC), BF16),
            pltpu.VMEM((1, CELLS), jnp.int32),
            pltpu.VMEM((CHILDREN, DP), F32),
            pltpu.VMEM((DC, DP), BF16),
            pltpu.VMEM((DBLOCKS, 8, WIDE + BAND), BF16),
            pltpu.SemaphoreType.DMA((2 * FRONT_TILES + 3,)),
        ],
        compiler_params=params(),
        cost_estimate=pl.CostEstimate(flops=2 * 128 * DC * DP, bytes_accessed=DC * DP * 2, transcendentals=0),
    )(*in_hbm(*args))


def cells_kernel(recv_ref, order_ref, sources_ref, edge_ref):
    core, half, chip = lax.axis_index("core"), lax.axis_index("dir_1"), lax.axis_index("chip")
    turned = jnp.where(core == 0, chip % RUN == 0, chip % RUN == RUN - 1).astype(jnp.int32)
    own = order_ref[...]
    ends = recv_ref[:16, WIDE:].astype(F32)
    mate = jnp.where(core == 0, ends[0:1], ends[8:9]).astype(jnp.int32)
    onehots = []
    for position, side, held in ((own, 1 - core, half), (mate, core, half ^ turned)):
        rows = (position >> 4) * 16 + side * 8 + (position & 7)
        rows = jnp.where(((position >> 3) & 1) == held, rows, -1)
        column = jnp.broadcast_to(rows.astype(F32), (BAND, BAND)).T.astype(jnp.int32)
        lanes = lax.broadcasted_iota(jnp.int32, (BAND, BAND), 1)
        onehots.append(jnp.where(column == lanes, 1.0, 0.0).astype(BF16))
    sources = jnp.dot(jnp.concatenate(onehots, axis=0), recv_ref[:, :WIDE], preferred_element_type=F32)
    sources_ref[...] = sources.astype(BF16)
    edge_ref[...] = jnp.where(core == 0, sources[CELLS - HALO : CELLS], sources[:HALO]).astype(BF16)


def to_cells(received, order):
    return pl.pallas_call(
        cells_kernel,
        in_specs=[whole()] * 2,
        out_specs=[whole()] * 2,
        out_shape=(
            jax.ShapeDtypeStruct((2 * CELLS, WIDE), BF16),
            jax.ShapeDtypeStruct((HALO, WIDE), BF16),
        ),
        compiler_params=params(),
    )(received, order)


def by_part_columns(ops):
    ops = ops.astype(F32)
    return jnp.concatenate([ops[:, 0], ops[:, 1]], axis=1).astype(BF16)


def onehot_rows(positions, width, first, rows):
    lanes = lax.broadcasted_iota(jnp.int32, (rows, width), 1)
    picks = [
        jnp.where(positions[first : first + rows, j : j + 1] == lanes, 1.0, 0.0).astype(BF16) for j in range(ENTRIES)
    ]
    return jnp.concatenate(picks, axis=0)


def added_up(fields, ops):
    re = jnp.zeros((GROUP, BAND), F32)
    im = re
    for j in range(ENTRIES):
        at = slice(j * GROUP, (j + 1) * GROUP)
        f, w = fields[at], ops[at]
        fr, fi, wr, wi = f[:, :BAND], f[:, BAND:], w[:, :BAND], w[:, BAND:]
        re = re + (wr * fr - wi * fi)
        im = im + (wr * fi + wi * fr)
    return jnp.concatenate([re, im], axis=1)


def translate_kernel(sources_ref, edge_ref, code_ref, index_ref, own_ref, other_ref, order_ref, out_ref):
    core, half = lax.axis_index("core"), lax.axis_index("dir_1")
    edge = edge_ref[...].astype(F32)
    outside = sources_ref[CELLS:].astype(F32)
    first = jnp.concatenate([edge, outside[HALO:]], axis=0)
    second = jnp.concatenate([outside[: CELLS - HALO], edge], axis=0)
    edges = jnp.where(core == 0, first, second).astype(BF16)
    sources = jnp.concatenate([sources_ref[:CELLS], edges], axis=0)
    low, high = sources[:, : 2 * BAND], sources[:, 2 * BAND :]
    own_ops, other_ops = by_part_columns(own_ref[...]), by_part_columns(other_ref[...])
    sides = (
        (low, jnp.where(half == 0, own_ops, other_ops)),
        (high, jnp.where(half == 0, other_ops, own_ops)),
    )

    code, index = code_ref[...], index_ref[...]
    cell = lax.broadcasted_iota(jnp.int32, code.shape, 0)
    up = (code * 37) >> 8
    u = (cell >> 4) + up - 3
    v = ((cell & 15) + code - 7 * up + (COLS - 3)) & 15
    source = (u & 7) * COLS + v + jnp.where((u < 0) | (u > 7), CELLS, 0)
    totals = []
    for k in range(CELLS // GROUP):
        picks = onehot_rows(source, 2 * CELLS, k * GROUP, GROUP)
        choices = onehot_rows(index, NOPS, k * GROUP, GROUP)
        both = []
        for fields, ops in sides:
            got = jnp.dot(picks, fields, preferred_element_type=F32)
            chosen = jnp.dot(choices, ops, preferred_element_type=F32)
            both.append(added_up(got, chosen))
        totals.append(jnp.concatenate(both, axis=1))
    translated = jnp.concatenate(totals, axis=0).astype(BF16)
    rows = lax.broadcasted_iota(jnp.int32, (CELLS, CELLS), 0)
    place = order_ref[...]
    place = ((place >> 3) & 1) * 64 + (place >> 4) * 8 + (place & 7)
    onehot = jnp.where(rows == place, 1.0, 0.0).astype(BF16)
    out_ref[...] = jnp.dot(onehot, translated, preferred_element_type=F32).astype(BF16)


def translate(*args):
    return pl.pallas_call(
        translate_kernel,
        in_specs=[whole()] * 7,
        out_specs=whole(),
        out_shape=jax.ShapeDtypeStruct((CELLS, WIDE), BF16),
        compiler_params=params(),
    )(*args)


def anterpolate_kernel(recv_ref, interp_ref, cos_ref, sin_ref, out_ref):
    total = jnp.zeros((128, DC), F32)
    per_tile = TILE // (2 * BAND)
    halves = recv_ref[...].astype(F32).reshape(2, 64, WIDE)
    for t in range(TILES):
        at = slice(t * TILE, (t + 1) * TILE)
        c, s = cos_ref[:, at], sin_ref[:, at]
        rows = slice(8 * per_tile * t, 8 * per_tile * (t + 1))
        values = halves[0, rows] + halves[1, rows]
        re, im = [], []
        for y in range(per_tile):
            both = values[8 * y : 8 * y + 8]
            re += [both[:, :BAND], both[:, 2 * BAND : 3 * BAND]]
            im += [both[:, BAND : 2 * BAND], both[:, 3 * BAND :]]
        re, im = jnp.concatenate(re, axis=1), jnp.concatenate(im, axis=1)
        real, imag = [], []
        for k in range(CHILDREN):
            ck, sk = c[k : k + 1], s[k : k + 1]
            real.append(ck * re + sk * im)
            imag.append(ck * im - sk * re)
        shifted = jnp.concatenate(real + imag, axis=0).astype(BF16)
        total += lax.dot_general(
            shifted, interp_ref[:, at], (((1,), (1,)), ((), ())), preferred_element_type=F32
        )
    rows = by_box((total * (DC / DP)).astype(BF16))
    out_ref[...] = rows.reshape(64, 2, DC)


def anterpolate(received, interp, c, s):
    return pl.pallas_call(
        anterpolate_kernel,
        in_specs=[whole()] * 4,
        out_specs=whole(),
        out_shape=jax.ShapeDtypeStruct((64, 2, DC), BF16),
        compiler_params=params(),
    )(received, interp, c, s)


def neighbour_groups(chips):
    groups = []
    for half in range(2):
        for chip in range(chips):
            there = half ^ 1 if chip % RUN == RUN - 1 else half
            sides = ((half * chips + chip) * 2 + 1, (there * chips + (chip + 1) % chips) * 2)
            groups.append([y * 4 * chips + side for y in range(DBLOCKS // 2) for side in sides])
    return groups


def patch_groups(chips):
    size = 2 * chips
    return [[(2 * y + half) * size + box for half in range(2) for y in range(DBLOCKS // 2)] for box in range(size)]


def other_half(chips):
    pairs = []
    for half in range(2):
        for chip in range(chips):
            for core in range(2):
                pairs.append(((half * chips + chip) * 2 + core, ((half ^ 1) * chips + (chip ^ 2)) * 2 + core))
    return pairs


def per_device(child_fields, interp_matrix, phase_angle, patch_order, offset_code, operator_index, operators):
    chips = lax.axis_size("chip")
    other = lax.ppermute(operators, ("dir_1", "chip", "core"), other_half(chips))
    send, c, s = front(child_fields.reshape(64, 2, DC), patch_order, phase_angle, interp_matrix)
    received = lax.all_to_all(
        send, DIR + ("chip", "core"), 0, 0, axis_index_groups=neighbour_groups(chips), tiled=True
    )
    index = operator_index.reshape(CELLS, ENTRIES)
    sources, edge = to_cells(received.reshape(CELLS, WIDE + BAND), patch_order)
    edge = lax.ppermute(edge, "core", [(0, 1), (1, 0)])
    returned = translate(sources, edge, offset_code.reshape(CELLS, ENTRIES), index, operators, other, patch_order)
    back = lax.all_to_all(
        returned.reshape(DBLOCKS, 8, WIDE), DIR + ("chip", "core"), 0, 0, axis_index_groups=patch_groups(chips), tiled=True
    )
    fields = anterpolate(back.reshape(8 * DBLOCKS, WIDE), interp_matrix, c, s)
    return fields.reshape(8, CHILDREN, 2, DC)


def solution(mesh):
    split = Mesh(mesh.devices.reshape(8, 2, mesh.shape["box"] // 2, 2), ("dir_0", "dir_1", "chip", "core"))
    box = ("chip", "core")
    placed = (
        P(box + DIR, None, None, None),
        P(),
        P(),
        P(box, None),
        P(box, None, None),
        P(box, None, None),
        P(None, None, DIR),
    )
    return jax.shard_map(
        per_device,
        mesh=split,
        in_specs=placed,
        out_specs=P(box + DIR, None, None, None),
        check_vma=False,
    )
```
